256 devices in a mesh: ctx: 64 (over x, z, core), dp: 4 (over y).
Axes of the slice: x: 4, y: 4, z: 8, core: 2. Of those that a mesh axis runs over, the one named last changes fastest.
Arguments:
- queries: bfloat16 [65536, 128], P(('dp', 'ctx')), parts along dimension 0, may hold values from -12 to 12
- keys: bfloat16 [65536, 128], P(('dp', 'ctx')), parts along dimension 0, may hold values from -4 to 4
- values: bfloat16 [65536, 128], P(('dp', 'ctx')), parts along dimension 0, may hold values from -6 to 6
- out_grad: bfloat16 [65536, 128], P(('dp', 'ctx')), parts along dimension 0, may hold values from -6 to 6
- segments: int32 [65536], P(('dp', 'ctx')), parts along dimension 0, may hold values from 0 to 11, never falling along the last dimension, each value on 1 to 10240 neighbouring positions
Outputs:
- attended: bfloat16 [65536, 128], P(('dp', 'ctx')), parts along dimension 0
- query_grad: bfloat16 [65536, 128], P(('dp', 'ctx')), parts along dimension 0
- key_grad: bfloat16 [65536, 128], P(('dp', 'ctx')), parts along dimension 0
- value_grad: bfloat16 [65536, 128], P(('dp', 'ctx')), parts along dimension 0
The draws below stay inside these ranges and needn't reach their ends.
There are 4 independent parts, one for each index of `dp`. The reference program is written for one: setup_inputs(seed, part) draws one part's arguments, and reference() takes and returns one part's arrays. A program takes and returns all parts, laid end to end along the dimension named above; each array names one. Nothing has to cross between parts.
Inputs may be any that keep to these rules, and one draw needn't show every extreme that they name: `segments`: ids never fall; every one of the 12 documents is present with 1 to 10240 tokens, one of exactly that many.
All inputs are finite; a program needn't handle non-finite values.
Results may differ from the reference program's by a relative error of at most 0.034.
Values may be sent and summed in bfloat16 or wider, within the bound.
A program may use at most 128 MiB of HBM per device.

```python
import math
import jax
import jax.numpy as jnp
import numpy as np
from jax import lax

HD = 128
DOCS = 12
SEQ = 16384


def draw_queries(key, part):
    key = jax.random.fold_in(key, 3)
    row_scale = jnp.exp(jax.random.uniform(jax.random.fold_in(key, 5), (SEQ, 1), jnp.float32, -1.2, 1.1))
    result = jax.random.normal(key, (SEQ, HD), jnp.float32) * row_scale
    return jnp.clip(result, -12.0, 12.0).astype(jnp.bfloat16)


def draw_keys(key, part):
    key = jax.random.fold_in(key, 11)
    result = jax.random.normal(key, (SEQ, HD), jnp.float32)
    return jnp.clip(result, -4.0, 4.0).astype(jnp.bfloat16)


def levels(own_key, extent, shards, low, largest):
    def one(position, parts):
        heights = jax.random.uniform(jax.random.fold_in(jax.random.fold_in(own_key, 6), position), (parts,), jnp.float32, low / len(shards), largest / len(shards))
        return jnp.repeat(jnp.exp(heights), extent[position] // parts).reshape((-1,) + (1,) * (len(extent) - position - 1))

    loudness = one(*shards[0])
    for cut in shards[1:]:
        loudness = loudness * one(*cut)
    return loudness


def length_profile(count, total, reach, skew):
    portions = [(1 << 20) // math.isqrt(standing ** skew) + 1 for standing in range(2, count + 1)]
    spare, given = total - reach - (count - 1), [1] * (count - 1)
    while spare > 0:
        candidates = [i for i in range(count - 1) if given[i] < reach]
        pool, budget = sum([portions[i] for i in candidates]), spare
        for i in candidates:
            addition = min(reach - given[i], max(1, budget * portions[i] // pool), spare)
            given[i] = given[i] + addition
            spare = spare - addition
    return np.array([reach] + given)


def uneven_parts(rng, number_of, total, reach, lean):
    if number_of == 2:
        one = jax.random.randint(rng, (), max(1, total - reach), min(reach, total - 1) + 1)
        return jnp.stack([one, total - one])
    sizes = jnp.asarray(length_profile(number_of, total, reach, lean), jnp.int32)
    twos = (number_of - 1) // 2
    donor, taker = sizes[1:1 + 2 * twos:2], sizes[2:2 + 2 * twos:2]
    room = jnp.minimum(donor - 1, reach - taker)
    passed = jax.random.randint(jax.random.fold_in(rng, 1), (twos,), 0, 1 << 20) % (room + 1)
    sizes = sizes.at[1:1 + 2 * twos:2].set(donor - passed).at[2:2 + 2 * twos:2].set(taker + passed)
    return sizes[jax.random.permutation(jax.random.fold_in(rng, 2), number_of)]


def noise(rng, dims, spread, limit, pieces=(), kind=jnp.bfloat16):
    level = levels(rng, dims, pieces, -0.22, 0.18) if pieces else 1.0
    values = jax.random.normal(rng, dims, jnp.float32) * spread * level
    return jnp.minimum(jnp.maximum(values, -limit), limit).astype(kind)


def setup_inputs(seed: int = 0, part: int = 0) -> dict:
    seeds = jax.random.split(jax.random.key(seed), 6)
    own_keys = jax.random.split(jax.random.fold_in(seeds[5], part), 6)
    queries = draw_queries(jax.random.fold_in(jax.random.fold_in(seeds[5], part), 71), part)
    keys = draw_keys(jax.random.fold_in(jax.random.fold_in(seeds[5], part), 71), part)
    values = noise(own_keys[2], (SEQ, HD), 1.0, 6.0, ((0, 64),))
    out_grad = noise(own_keys[3], (SEQ, HD), 1.0, 6.0, ((0, 64),))
    segments = jnp.searchsorted(jnp.cumsum(uneven_parts(own_keys[4], DOCS, SEQ, SEQ * 5 // 8, 2)), jnp.arange(SEQ), side="right").astype(jnp.int32)
    return {"queries": queries, "keys": keys, "values": values, "out_grad": out_grad, "segments": segments}


masked_score = -1e+30

def bounds(segments):
    labels = jnp.arange(DOCS, dtype=jnp.int32)
    one_hot = (segments[:, None] == labels[None, :]).astype(jnp.int32)
    counts = lax.optimization_barrier(jnp.sum(one_hot, axis=0)).astype(jnp.int32)
    starts = (jnp.cumsum(counts) - counts).astype(jnp.int32)
    doc_first = lax.optimization_barrier(jnp.sum(one_hot * starts[None, :], axis=1)).astype(jnp.int32)
    doc_end = doc_first + lax.optimization_barrier(jnp.sum(one_hot * counts[None, :], axis=1)).astype(jnp.int32)
    return (doc_first, doc_end)

def reference(queries, keys, values, out_grad, segments):
    inv_root = 1.0 / math.sqrt(HD)
    block_rows = math.gcd(SEQ, 1024)
    blocks = SEQ // block_rows
    doc_first, doc_end = bounds(segments)
    positions = jnp.arange(SEQ, dtype=jnp.int32)

    def forward_block(block_index):
        offset = (block_index * block_rows).astype(jnp.int32)
        query_rows = lax.dynamic_slice_in_dim(queries, offset, block_rows, 0)
        firsts = lax.dynamic_slice_in_dim(doc_first, offset, block_rows, 0)
        query_pos = offset + jnp.arange(block_rows, dtype=jnp.int32)
        scores = jnp.dot(query_rows, keys.T, preferred_element_type=jnp.float32) * inv_root
        allowed = (positions[None, :] <= query_pos[:, None]) & (positions[None, :] >= firsts[:, None])
        row_max = lax.optimization_barrier(jnp.max(jnp.where(allowed, scores, masked_score), axis=1))
        exps = jnp.where(allowed, jnp.exp(scores - row_max[:, None]), 0.0)
        totals = lax.optimization_barrier(jnp.sum(exps, axis=1))
        mixed = jnp.dot(exps.astype(jnp.bfloat16), values, preferred_element_type=jnp.float32)
        return ((mixed / totals[:, None]).astype(jnp.bfloat16), row_max + jnp.log(totals))
    attended, log_total = lax.map(forward_block, jnp.arange(blocks, dtype=jnp.int32))
    attended = attended.reshape(SEQ, HD)
    log_total = log_total.reshape(SEQ)
    row_delta = lax.optimization_barrier(jnp.sum(out_grad.astype(jnp.float32) * attended.astype(jnp.float32), axis=1))

    def query_block(block_index):
        offset = (block_index * block_rows).astype(jnp.int32)
        query_rows = lax.dynamic_slice_in_dim(queries, offset, block_rows, 0)
        grad_rows = lax.dynamic_slice_in_dim(out_grad, offset, block_rows, 0)
        firsts = lax.dynamic_slice_in_dim(doc_first, offset, block_rows, 0)
        total_rows = lax.dynamic_slice_in_dim(log_total, offset, block_rows, 0)
        delta_rows = lax.dynamic_slice_in_dim(row_delta, offset, block_rows, 0)
        query_pos = offset + jnp.arange(block_rows, dtype=jnp.int32)
        scores = jnp.dot(query_rows, keys.T, preferred_element_type=jnp.float32) * inv_root
        allowed = (positions[None, :] <= query_pos[:, None]) & (positions[None, :] >= firsts[:, None])
        probs = jnp.where(allowed, jnp.exp(scores - total_rows[:, None]), 0.0)
        prob_grad = jnp.dot(grad_rows, values.T, preferred_element_type=jnp.float32)
        score_grad = (probs * (prob_grad - delta_rows[:, None]) * inv_root).astype(jnp.bfloat16)
        return jnp.dot(score_grad, keys, preferred_element_type=jnp.float32).astype(jnp.bfloat16)
    query_grad = lax.map(query_block, jnp.arange(blocks, dtype=jnp.int32)).reshape(SEQ, HD)

    def key_block(block_index):
        offset = (block_index * block_rows).astype(jnp.int32)
        key_rows = lax.dynamic_slice_in_dim(keys, offset, block_rows, 0)
        value_rows = lax.dynamic_slice_in_dim(values, offset, block_rows, 0)
        ends = lax.dynamic_slice_in_dim(doc_end, offset, block_rows, 0)
        key_pos = offset + jnp.arange(block_rows, dtype=jnp.int32)
        scores = jnp.dot(queries, key_rows.T, preferred_element_type=jnp.float32) * inv_root
        allowed = (positions[:, None] >= key_pos[None, :]) & (positions[:, None] < ends[None, :])
        probs = jnp.where(allowed, jnp.exp(scores - log_total[:, None]), 0.0)
        value_part = jnp.dot(probs.astype(jnp.bfloat16).T, out_grad, preferred_element_type=jnp.float32)
        prob_grad = jnp.dot(out_grad, value_rows.T, preferred_element_type=jnp.float32)
        score_grad = (probs * (prob_grad - row_delta[:, None]) * inv_root).astype(jnp.bfloat16)
        key_part = jnp.dot(score_grad.T, queries, preferred_element_type=jnp.float32)
        return (key_part.astype(jnp.bfloat16), value_part.astype(jnp.bfloat16))
    key_grad, value_grad = lax.map(key_block, jnp.arange(blocks, dtype=jnp.int32))
    return (attended, query_grad, key_grad.reshape(SEQ, HD), value_grad.reshape(SEQ, HD))
```

```python
import functools
import math

import jax
import jax.numpy as jnp
from jax import lax
from jax.experimental import pallas as pl
from jax.experimental.pallas import tpu as pltpu
from jax.sharding import PartitionSpec as P

MESH = pl.DeviceIdType.MESH
HD = 128
X, Z = 4, 8
T = 256
C = 2 * T
SEG_ROWS = 16
NEG = -1e30
INV_ROOT = 1.0 / math.sqrt(HD)
ALPHA = INV_ROOT * math.log2(math.e)
F32 = jnp.float32
BF16 = jnp.bfloat16
NT = (((1,), (1,)), ((), ()))


def kernel(
    q_ref, k_ref, v_ref, g_ref, seg_ref,
    att_ref, dq_ref, dk_ref, dv_ref,
    qs, gs, ks, vs, kt, vt, eb, dp, pb, db, acc, kacc, cnt,
    sts, str_, fin, zs, zr, sbs, sbr, xs, xr,
    zq_s, zq_r, zg_s, zg_r, kv_s, kv_r, st_s, st_r, fn_s, fn_r,
    za_s, za_r, sb_s, sb_r, xr_s, xr_r,
):
    ctx = lax.axis_index("ctx")
    x = ctx // (2 * Z)
    z = (ctx // 2) % Z
    core = ctx % 2

    def dev(xx, zz, cc):
        return {"ctx": ((xx + X) % X) * (2 * Z) + ((zz + Z) % Z) * 2 + cc}

    sib = dev(x, z, 1 - core)
    z_right, z_left = dev(x, z + 1, core), dev(x, z - 1, core)
    x_right, x_left = dev(x + 1, z, core), dev(x - 1, z, core)

    barrier = pltpu.get_barrier_semaphore()
    for r in range(1, Z):
        pl.semaphore_signal(barrier, inc=1, device_id=dev(x, z - r, core), device_id_type=MESH)
    for peer in (sib, x_right, x_left):
        pl.semaphore_signal(barrier, inc=1, device_id=peer, device_id_type=MESH)

    qs[0, 0:T, :] = q_ref[...]
    qs[0, T : T + SEG_ROWS, :] = seg_ref[...]
    gs[0] = g_ref[...]
    ks[0, core, 0:T, :] = k_ref[...]
    ks[0, core, T : T + SEG_ROWS, :] = seg_ref[...]
    vs[0, core] = v_ref[...]

    pl.semaphore_wait(barrier, Z + 2)

    started = []

    def copy(src, dst, send, recv, target):
        return pltpu.make_async_remote_copy(
            src_ref=src, dst_ref=dst, send_sem=send, recv_sem=recv,
            device_id=target, device_id_type=MESH,
        )

    def send(op):
        op.start()
        started.append(op)

    def q_hop(src, dst, target):
        return copy(qs.at[src], qs.at[dst], zq_s.at[dst], zq_r.at[dst], target)

    def g_hop(src, dst, target):
        return copy(gs.at[src], gs.at[dst], zg_s.at[dst], zg_r.at[dst], target)

    def k_hop(i, src, dst, target):
        return copy(ks.at[src, core], ks.at[dst, core], kv_s.at[i], kv_r.at[i], target)

    def v_hop(i, src, dst, target):
        return copy(vs.at[src, core], vs.at[dst, core], kv_s.at[i], kv_r.at[i], target)

    q_right = [q_hop(j, j + 1, z_right) for j in range(4)]
    q_left = [q_hop((8 - j) % 8, 7 - j, z_left) for j in range(3)]
    g_right = [g_hop(j, j + 1, z_right) for j in range(3)]
    g_left = [g_hop((8 - j) % 8, 7 - j, z_left) for j in range(4)]
    k_sib = {0: k_hop(0, 0, 0, sib), 1: k_hop(1, 1, 1, sib), 2: k_hop(2, 2, 2, sib), 3: k_hop(3, 3, 3, sib)}
    v_sib = {0: v_hop(4, 0, 0, sib), 1: v_hop(5, 1, 1, sib), 2: v_hop(6, 2, 2, sib), 3: v_hop(7, 3, 3, sib)}
    k_right, v_right = k_hop(8, 0, 1, x_right), v_hop(9, 0, 1, x_right)
    k_left, v_left = k_hop(10, 0, 3, x_left), v_hop(11, 0, 3, x_left)
    k_far, v_far = k_hop(12, 1, 2, x_right), v_hop(13, 3, 2, x_left)

    for op in (q_right[0], q_left[0], k_right, k_left, g_right[0], g_left[0], v_right, v_left, k_sib[0], v_sib[0]):
        send(op)

    def z_step(j):
        q_right[j - 1].wait_recv()
        if j < 4:
            q_right[j].start()
            q_left[j - 1].wait_recv()
        if j < 3:
            q_left[j].start()
        g_left[j - 1].wait_recv()
        if j < 4:
            g_left[j].start()
            g_right[j - 1].wait_recv()
        if j < 3:
            g_right[j].start()

    z_step(1)
    k_right.wait_recv()
    send(k_far)
    send(k_sib[1])
    v_left.wait_recv()
    send(v_far)
    send(v_sib[3])
    v_right.wait_recv()
    send(v_sib[1])
    k_left.wait_recv()
    send(k_sib[3])
    k_far.wait_recv()
    send(k_sib[2])
    v_far.wait_recv()
    send(v_sib[2])
    for s in range(X):
        k_sib[s].wait_recv()
        v_sib[s].wait_recv()
    z_step(2)

    doc16 = lax.broadcasted_iota(jnp.int32, (16, HD), 0).astype(F32)

    def prepare(s, _):
        below = jnp.zeros((16, HD), F32)
        for c in range(2):
            kt[s, :, c * T : (c + 1) * T] = ks[s, c, 0:T, :].T
            vt[s, :, c * T : (c + 1) * T] = vs[s, c].T
            seg = ks[s, c, T : T + SEG_ROWS, :].astype(F32)
            for h in range(T // HD):
                below += jnp.where(seg[h : h + 1, :] < doc16, 1.0, 0.0)
        cnt[s] = jnp.broadcast_to(jnp.sum(below, axis=1, keepdims=True), (16, T))
        return 0

    lax.fori_loop(0, X, prepare, 0)

    def slots(r):
        own = (r == 0) | (r > z)
        used = own | ((x == X - 1) & (r >= 4))
        return jnp.where(used, 0, 1), jnp.where(own, 0, 3), jnp.minimum(x, 2) + 1

    key_row = lax.broadcasted_iota(jnp.int32, (T, T), 0).astype(F32)
    query_lane = lax.broadcasted_iota(jnp.int32, (1, T), 1).astype(F32)
    doc_q = lax.broadcasted_iota(jnp.int32, (16, T), 0).astype(F32)

    def stat_send(r):
        return copy(sts.at[r], str_.at[r], st_s.at[r], st_r.at[r], dev(x, z - r, core))

    def first(i, _):
        @pl.when(i == 3)
        def _():
            z_step(3)

        @pl.when(i == 5)
        def _():
            z_step(4)

        r = jnp.where(i % 2 == 1, (i + 1) // 2, (8 - i // 2) % 8)
        u_low, s_zero, u_high = slots(r)
        seg = qs[r, T : T + SEG_ROWS, :].astype(F32)
        seg_q = jnp.concatenate([seg[0:1, :], seg[1:2, :]], axis=1)
        same = seg_q == doc_q

        def scores(u, top):
            s = jnp.where(u == 0, s_zero, u)
            low = jnp.sum(jnp.where(same, cnt[s], 0.0), axis=0, keepdims=True)
            diagonal = (s == 0) & (r == 0)
            high = jnp.where(diagonal, query_lane + (core * T).astype(F32), 1e9)
            for c in range(2):
                sc = lax.dot_general(ks[s, c, 0:T, :], qs[r, 0:T, :], NT, preferred_element_type=F32)
                pos = key_row + c * T
                sc = jnp.where((pos >= low) & (pos <= high), sc, NEG)
                eb[r, u, c * T : (c + 1) * T, :] = sc
                top = jnp.maximum(top, jnp.max(sc, axis=0, keepdims=True))
            return top

        top = lax.fori_loop(u_low, u_high, scores, jnp.full((1, T), NEG, F32))

        def exps(u, sums):
            total, moment = sums
            s = jnp.where(u == 0, s_zero, u)
            for c in range(2):
                rows = slice(c * T, (c + 1) * T)
                e = jnp.exp2((eb[r, u, rows, :] - top) * ALPHA)
                eb[r, u, rows, :] = e
                grad = lax.dot_general(vs[s, c], gs[r], NT, preferred_element_type=F32)
                dp[r, u, rows, :] = grad
                total += jnp.sum(e, axis=0, keepdims=True)
                moment += jnp.sum(e * grad, axis=0, keepdims=True)
            return total, moment

        zero = jnp.zeros((1, T), F32)
        total, moment = lax.fori_loop(u_low, u_high, exps, (zero, zero))
        sts[r, 0:1, :] = top
        sts[r, 1:2, :] = total
        sts[r, 2:3, :] = moment

        @pl.when(i > 0)
        def _():
            stat_send(r).start()

        return 0

    lax.fori_loop(0, Z, first, 0)

    for r in range(1, Z):
        stat_send(r).wait_recv()
    tops = [sts[0, 0:1, :]] + [str_[r, 0:1, :] for r in range(1, Z)]
    top = functools.reduce(jnp.maximum, tops)
    total = jnp.zeros((1, T), F32)
    moment = jnp.zeros((1, T), F32)
    for r in range(Z):
        box = sts if r == 0 else str_
        scale = jnp.exp2((tops[r] - top) * ALPHA)
        total += box[r, 1:2, :] * scale
        moment += box[r, 2:3, :] * scale
    inverse = 1.0 / total
    fin[0, 0:1, :] = top
    fin[0, 1:2, :] = inverse
    fin[0, 2:3, :] = moment * inverse

    def fin_send(r):
        return copy(fin.at[0], fin.at[r], fn_s.at[r], fn_r.at[r], dev(x, z + r, core))

    for r in (4, 3, 5, 2, 6, 1, 7):
        send(fin_send(r))

    def z_sum(d, i, what):
        return copy(
            zs.at[d, i, what], zr.at[d, i, what], za_s.at[d, i, what], za_r.at[d, i, what],
            z_right if d == 0 else z_left,
        )

    def z_add(i):
        for d in range(2):
            r = 4 + i if d == 0 else 4 - i
            for what in range(2):
                part = acc[r, what]
                if i > 1 or what == d:
                    z_sum(d, i - 1, what).wait_recv()
                    part = part + zr[d, i - 1, what].astype(F32)
                zs[d, i, what] = part.astype(BF16)
                send(z_sum(d, i, what))

    def second(i, _):
        @pl.when(i == 1)
        def _():
            for d in range(2):
                zs[d, 0, d] = acc[4, d].astype(BF16)
                z_sum(d, 0, d).start()

        r = jnp.where(i % 2 == 1, (4 + (i + 1) // 2) % 8, 4 - i // 2)

        @pl.when(r > 0)
        def _():
            fin_send(r).wait_recv()

        u_low, s_zero, u_high = slots(r)
        scale = jnp.exp2((sts[r, 0:1, :] - fin[r, 0:1, :]) * ALPHA) * fin[r, 1:2, :]
        delta = fin[r, 2:3, :]
        root_scale = scale * INV_ROOT
        acc[r] = jnp.zeros((2, HD, T), F32)
        lanes = pl.ds(pl.multiple_of(r * T, T), T)

        def body(u, _):
            s = jnp.where(u == 0, s_zero, u)
            e = eb[r, u]
            p = (e * scale).astype(BF16)
            ds = (e * root_scale * (dp[r, u] - delta)).astype(BF16)
            pb[u, :, lanes] = p
            db[u, :, lanes] = ds
            acc[r, 0] += jnp.dot(vt[s], p, preferred_element_type=F32)
            acc[r, 1] += jnp.dot(kt[s], ds, preferred_element_type=F32)
            return 0

        lax.fori_loop(u_low, u_high, body, 0)
        return 0

    lax.fori_loop(0, Z, second, 0)
    z_add(1)

    def sib_send(s):
        return copy(sbs.at[s], sbr.at[s], sb_s.at[s], sb_r.at[s], sib)

    def key_part(s, u, r_low, r_high):
        kacc[s] = jnp.zeros((2, C, HD), F32)

        def body(i, _):
            r = i % Z
            lanes = pl.ds(pl.multiple_of(r * T, T), T)
            kacc[s, 0] += jnp.dot(db[u, :, lanes], qs[r, 0:T, :], preferred_element_type=F32)
            kacc[s, 1] += jnp.dot(pb[u, :, lanes], gs[r], preferred_element_type=F32)
            return 0

        lax.fori_loop(r_low, r_high, body, 0)
        other = pl.ds(pl.multiple_of((1 - core) * T, T), T)
        for what in range(2):
            sbs[s, what] = kacc[s, what, other, :].astype(BF16)
        send(sib_send(s))

    mine = pl.ds(pl.multiple_of(core * T, T), T)

    def own_part(s, what):
        return kacc[s, what, mine, :] + sbr[s, what].astype(F32)

    x_target = [x_right, x_left, x_left, x_left, x_right, x_right]

    def x_sum(i):
        return copy(xs.at[i], xr.at[i], xr_s.at[i], xr_r.at[i], x_target[i])

    key_part(2, 2, 0, jnp.where(x >= 2, Z, 0))
    key_part(1, 1, 0, jnp.where(x >= 1, Z, 0))
    z_add(2)
    sib_send(2).wait_recv()
    for what in range(2):
        xs[what] = own_part(2, what).astype(BF16)
        send(x_sum(what))
    key_part(3, 0, 4, jnp.where(x == X - 1, z + 1, 4))
    key_part(0, 0, z + 1, Z + 1)
    z_add(3)
    sib_send(1).wait_recv()
    xs[2] = own_part(1, 0).astype(BF16)
    send(x_sum(2))
    x_sum(1).wait_recv()
    xs[3] = (own_part(1, 1) + xr[1].astype(F32)).astype(BF16)
    send(x_sum(3))
    sib_send(3).wait_recv()
    xs[5] = own_part(3, 1).astype(BF16)
    send(x_sum(5))
    x_sum(0).wait_recv()
    xs[4] = (own_part(3, 0) + xr[0].astype(F32)).astype(BF16)
    send(x_sum(4))

    sib_send(0).wait_recv()
    for i in (2, 5, 3, 4):
        x_sum(i).wait_recv()
    dk_ref[...] = (own_part(0, 0) + xr[2].astype(F32) + xr[4].astype(F32)).astype(BF16)
    dv_ref[...] = (own_part(0, 1) + xr[3].astype(F32) + xr[5].astype(F32)).astype(BF16)

    for what, out in ((0, att_ref), (1, dq_ref)):
        part = acc[0, what]
        for d in range(2):
            z_sum(d, 3, what).wait_recv()
            part = part + zr[d, 3, what].astype(F32)
        out[...] = part.T.astype(BF16)

    for op in started:
        op.wait_send()
    for ops in (q_right[1:], q_left[1:], g_right[1:], g_left[1:]):
        for op in ops:
            op.wait_send()
    for r in range(1, Z):
        stat_send(r).wait_send()
    for d in range(2):
        z_sum(d, 0, d).wait_send()


def per_device(queries, keys, values, out_grad, segments):
    seg = segments.astype(BF16).reshape(T // HD, HD)
    seg = jnp.pad(seg, ((0, SEG_ROWS - T // HD), (0, 0)))
    tile = jax.ShapeDtypeStruct((T, HD), BF16)
    vmem = pl.BlockSpec(memory_space=pltpu.VMEM)
    dma = pltpu.SemaphoreType.DMA
    return pl.pallas_call(
        kernel,
        out_shape=(tile,) * 4,
        in_specs=[vmem] * 5,
        out_specs=(vmem,) * 4,
        scratch_shapes=[
            pltpu.VMEM((Z, T + SEG_ROWS, HD), BF16),
            pltpu.VMEM((Z, T, HD), BF16),
            pltpu.VMEM((X, 2, T + SEG_ROWS, HD), BF16),
            pltpu.VMEM((X, 2, T, HD), BF16),
            pltpu.VMEM((X, HD, C), BF16),
            pltpu.VMEM((X, HD, C), BF16),
            pltpu.VMEM((Z, 3, C, T), F32),
            pltpu.VMEM((Z, 3, C, T), F32),
            pltpu.VMEM((3, C, Z * T), BF16),
            pltpu.VMEM((3, C, Z * T), BF16),
            pltpu.VMEM((Z, 2, HD, T), F32),
            pltpu.VMEM((X, 2, C, HD), F32),
            pltpu.VMEM((X, 16, T), F32),
            pltpu.VMEM((Z, 8, T), F32),
            pltpu.VMEM((Z, 8, T), F32),
            pltpu.VMEM((Z, 8, T), F32),
            pltpu.VMEM((2, 4, 2, HD, T), BF16),
            pltpu.VMEM((2, 4, 2, HD, T), BF16),
            pltpu.VMEM((X, 2, T, HD), BF16),
            pltpu.VMEM((X, 2, T, HD), BF16),
            pltpu.VMEM((6, T, HD), BF16),
            pltpu.VMEM((6, T, HD), BF16),
            dma((Z,)), dma((Z,)), dma((Z,)), dma((Z,)),
            dma((14,)), dma((14,)),
            dma((Z,)), dma((Z,)), dma((Z,)), dma((Z,)),
            dma((2, 4, 2)), dma((2, 4, 2)),
            dma((X,)), dma((X,)), dma((6,)), dma((6,)),
        ],
        compiler_params=pltpu.CompilerParams(
            collective_id=0, has_side_effects=True, vmem_limit_bytes=58 * 1024 * 1024
        ),
        cost_estimate=pl.CostEstimate(
            flops=4 * 10**9, bytes_accessed=600_000, transcendentals=2 * 10**6
        ),
    )(queries, keys, values, out_grad, seg)


def solution(mesh):
    rows = P(("dp", "ctx"), None)
    return jax.shard_map(
        per_device,
        mesh=mesh,
        in_specs=(rows, rows, rows, rows, P(("dp", "ctx"))),
        out_specs=(rows, rows, rows, rows),
        check_vma=False,
    )
```

```python
import functools
import math

import jax
import jax.numpy as jnp
from jax import lax
from jax.experimental import pallas as pl
from jax.experimental.pallas import tpu as pltpu
from jax.sharding import PartitionSpec as P

MESH = pl.DeviceIdType.MESH
HD = 128
X, Z = 4, 8
T = 256
C = 2 * T
SEG_ROWS = 16
NEG = -1e30
INV_ROOT = 1.0 / math.sqrt(HD)
ALPHA = INV_ROOT * math.log2(math.e)
F32 = jnp.float32
BF16 = jnp.bfloat16
NT = (((1,), (1,)), ((), ()))


def dot_nt(a, b):
    return lax.dot_general(a, b, NT, preferred_element_type=F32)


def dot(a, b):
    return jnp.dot(a, b, preferred_element_type=F32)


def pick(index, values):
    result = values[-1]
    for i in range(len(values) - 2, -1, -1):
        result = jnp.where(index == i, values[i], result)
    return result


def kernel(
    q_ref, k_ref, v_ref, g_ref, seg_ref, out_ref,
    segf, qs, gs, qt, gt, ks, vs, vkt, eb, tb, pst, run, accv, accw, kacc, cnt,
    str_, fin, zs, zr, sbs, sbr, xs, xr,
    zq_s, zq_r, zg_s, zg_r, kv_s, kv_r, st_s, st_r, fn_s, fn_r,
    za_s, za_r, sb_s, sb_r, xr_s, xr_r,
):
    ctx = lax.axis_index("ctx")
    x = ctx // (2 * Z)
    z = (ctx // 2) % Z
    core = ctx % 2

    def dev(xx, zz, cc):
        return {"ctx": ((xx + X) % X) * (2 * Z) + ((zz + Z) % Z) * 2 + cc}

    sib = dev(x, z, 1 - core)
    z_right, z_left = dev(x, z + 1, core), dev(x, z - 1, core)
    x_right, x_left = dev(x + 1, z, core), dev(x - 1, z, core)

    barrier = pltpu.get_barrier_semaphore()
    for peer in (z_right, z_left, x_right, x_left, sib):
        pl.semaphore_signal(barrier, inc=1, device_id=peer, device_id_type=MESH)

    segf[...] = jnp.zeros_like(segf)
    segf[0 : T // HD, :] = seg_ref[...].astype(F32)
    seg_rows = segf[...].astype(BF16)
    qs[0, 0:T, :] = q_ref[...]
    qs[0, T : T + SEG_ROWS, :] = seg_rows
    gs[0] = g_ref[...]
    ks[0, core, 0:T, :] = k_ref[...]
    ks[0, core, T : T + SEG_ROWS, :] = seg_rows
    vs[0, core] = v_ref[...]

    pl.semaphore_wait(barrier, 5)

    started = []

    def copy(src, dst, send, recv, target):
        return pltpu.make_async_remote_copy(
            src_ref=src, dst_ref=dst, send_sem=send, recv_sem=recv,
            device_id=target, device_id_type=MESH,
        )

    def send(op):
        op.start()
        started.append(op)

    def q_hop(src, dst, target):
        return copy(qs.at[src], qs.at[dst], zq_s.at[dst], zq_r.at[dst], target)

    def g_hop(src, dst, target):
        return copy(gs.at[src], gs.at[dst], zg_s.at[dst], zg_r.at[dst], target)

    def k_hop(i, src, dst, target):
        return copy(ks.at[src, core], ks.at[dst, core], kv_s.at[i], kv_r.at[i], target)

    def v_hop(i, src, dst, target):
        return copy(vs.at[src, core], vs.at[dst, core], kv_s.at[i], kv_r.at[i], target)

    q_right = [q_hop(j, j + 1, z_right) for j in range(4)]
    q_left = [q_hop((8 - j) % 8, 7 - j, z_left) for j in range(3)]
    g_right = [g_hop(j, j + 1, z_right) for j in range(3)]
    g_left = [g_hop((8 - j) % 8, 7 - j, z_left) for j in range(4)]
    k_sib = [k_hop(s, s, s, sib) for s in range(4)]
    v_sib = [v_hop(4 + s, s, s, sib) for s in range(4)]
    k_right, v_right = k_hop(8, 0, 1, x_right), v_hop(9, 0, 1, x_right)
    k_left, v_left = k_hop(10, 0, 3, x_left), v_hop(11, 0, 3, x_left)
    k_far, v_far = k_hop(12, 1, 2, x_right), v_hop(13, 3, 2, x_left)

    for op in (
        q_right[0], q_left[0], k_sib[0], v_sib[0], k_right, k_left,
        g_right[0], g_left[0], v_right, v_left,
    ):
        op.start()

    def z_step(j):
        q_right[j - 1].wait_recv()
        if j < 4:
            q_right[j].start()
            q_left[j - 1].wait_recv()
        if j < 3:
            q_left[j].start()
        g_left[j - 1].wait_recv()
        if j < 4:
            g_left[j].start()
            g_right[j - 1].wait_recv()
        if j < 3:
            g_right[j].start()

    doc16 = lax.broadcasted_iota(jnp.int32, (16, HD), 0).astype(F32)

    def prepare_keys(s):
        below = jnp.zeros((16, HD), F32)
        for c in range(2):
            vkt[s, 0:HD, c * T : (c + 1) * T] = vs[s, c].T
            vkt[s, HD:, c * T : (c + 1) * T] = ks[s, c, 0:T, :].T
            seg = ks[s, c, T : T + SEG_ROWS, :].astype(F32)
            for h in range(T // HD):
                below += jnp.where(seg[h : h + 1, :] < doc16, 1.0, 0.0)
        cnt[s] = jnp.broadcast_to(jnp.sum(below, axis=1, keepdims=True), (16, T))

    def prepare_queries(r):
        qt[r] = qs[r, 0:T, :].T
        gt[r] = gs[r].T

    key_row = lax.broadcasted_iota(jnp.int32, (T, T), 0).astype(F32)
    query_lane = lax.broadcasted_iota(jnp.int32, (1, T), 1).astype(F32)
    doc_q = lax.broadcasted_iota(jnp.int32, (16, T), 0).astype(F32)

    def slots(r):
        own = (r == 0) | (r > z)
        used = own | ((x == X - 1) & (r >= 4))
        return jnp.where(used, 0, 1), jnp.where(own, 0, 3), jnp.minimum(x, 2) + 1

    def piece(r, u, s):
        seg = qs[r, T : T + SEG_ROWS, :].astype(F32)
        seg_q = jnp.concatenate([seg[0:1, :], seg[1:2, :]], axis=1)
        low = jnp.sum(jnp.where(seg_q == doc_q, cnt[s], 0.0), axis=0, keepdims=True)
        diagonal = (s == 0) & (r == 0)
        high = jnp.where(diagonal, query_lane + (core * T).astype(F32), 1e9)
        q = qs[r, 0:T, :]
        g = gs[r]
        scores = []
        for c in range(2):
            sc = dot_nt(ks[s, c, 0:T, :], q)
            pos = key_row + c * T
            scores.append(jnp.where((pos >= low) & (pos <= high), sc, NEG))
        top = jnp.max(jnp.maximum(scores[0], scores[1]), axis=0, keepdims=True)
        exps = [jnp.exp2((sc - top) * ALPHA) for sc in scores]
        grads = [dot_nt(vs[s, c], g) for c in range(2)]
        total = jnp.sum(exps[0] + exps[1], axis=0, keepdims=True)
        moment = jnp.sum(exps[0] * grads[0] + exps[1] * grads[1], axis=0, keepdims=True)
        mean = moment / total
        for c in range(2):
            rows = slice(c * T, (c + 1) * T)
            eb[r, u, rows, :] = exps[c].astype(BF16)
            tb[r, u, rows, :] = (exps[c] * (grads[c] - mean)).astype(BF16)
        part_v = dot(vkt[s], eb[r, u])
        part_t = dot(vkt[s, HD:, :], tb[r, u])
        pst[r, u, 0:1, :] = top
        pst[r, u, 1:2, :] = mean
        old = run[r, 0:1, :]
        new = jnp.maximum(old, top)
        keep = jnp.exp2((old - new) * ALPHA)
        add = jnp.exp2((top - new) * ALPHA)
        run[r, 0:1, :] = new
        run[r, 1:2, :] = run[r, 1:2, :] * keep + total * add
        run[r, 2:3, :] = run[r, 2:3, :] * keep + moment * add
        accv[r] = accv[r] * keep + part_v * add
        accw[r] = accw[r] * keep + (part_t + mean * part_v[HD:, :]) * add

    def stat_send(r):
        return copy(run.at[r], str_.at[r], st_s.at[r], st_r.at[r], dev(x, z - r, core))

    def clear(r, _):
        run[r, 0:1, :] = jnp.full((1, T), NEG, F32)
        run[r, 1:8, :] = jnp.zeros((7, T), F32)
        accv[r] = jnp.zeros((2 * HD, T), F32)
        accw[r] = jnp.zeros((HD, T), F32)
        return 0

    lax.fori_loop(0, Z, clear, 0)

    def wave(w, _):
        @pl.when(w == 0)
        def _():
            prepare_queries(0)
            k_sib[0].wait_recv()
            v_sib[0].wait_recv()
            prepare_keys(0)

        @pl.when(w == 1)
        def _():
            q_right[0].wait_recv()
            q_right[1].start()
            q_left[0].wait_recv()
            q_left[1].start()
            k_right.wait_recv()
            k_far.start()
            k_sib[1].start()
            k_left.wait_recv()
            k_sib[3].start()
            g_left[0].wait_recv()
            g_left[1].start()
            g_right[0].wait_recv()
            g_right[1].start()
            v_left.wait_recv()
            v_far.start()
            v_sib[3].start()
            v_right.wait_recv()
            v_sib[1].start()
            prepare_queries(1)
            prepare_queries(7)
            k_sib[1].wait_recv()
            v_sib[1].wait_recv()
            prepare_keys(1)
            k_sib[3].wait_recv()
            v_sib[3].wait_recv()
            prepare_keys(3)

        @pl.when(w == 2)
        def _():
            z_step(2)
            k_far.wait_recv()
            k_sib[2].start()
            v_far.wait_recv()
            v_sib[2].start()
            prepare_queries(2)
            prepare_queries(6)

        @pl.when(w == 3)
        def _():
            k_sib[2].wait_recv()
            v_sib[2].wait_recv()
            prepare_keys(2)

        @pl.when(w == 4)
        def _():
            z_step(3)
            prepare_queries(3)
            prepare_queries(5)

        @pl.when(w == 5)
        def _():
            z_step(4)
            prepare_queries(4)

        i_low, i_high = pick(w, [0, 0, 3, 0, 5, 7]), pick(w, [1, 3, 5, 5, 7, 8])
        u_from, u_to = pick(w, [0, 0, 0, 2, 0, 0]), pick(w, [1, 2, 2, 3, 3, 3])

        def block(i, _):
            r = jnp.where(i % 2 == 1, (i + 1) // 2, (8 - i // 2) % 8)
            u_low, s_zero, u_high = slots(r)
            u_first = jnp.where((w == 1) & (i == 0), 1, u_from)

            def body(u, _):
                piece(r, u, jnp.where(u == 0, s_zero, u))
                return 0

            lax.fori_loop(jnp.maximum(u_low, u_first), jnp.minimum(u_high, u_to), body, 0)

            @pl.when((w >= 3) & (r > 0))
            def _():
                stat_send(r).start()

            return 0

        lax.fori_loop(i_low, i_high, block, 0)
        return 0

    lax.fori_loop(0, 6, wave, 0)

    for r in (1, 7, 2, 6, 3, 5, 4):
        stat_send(r).wait_recv()
    tops = [run[0, 0:1, :]] + [str_[r, 0:1, :] for r in range(1, Z)]
    top = functools.reduce(jnp.maximum, tops)
    total = jnp.zeros((1, T), F32)
    moment = jnp.zeros((1, T), F32)
    for r in range(Z):
        box = run if r == 0 else str_
        scale = jnp.exp2((tops[r] - top) * ALPHA)
        total += box[r, 1:2, :] * scale
        moment += box[r, 2:3, :] * scale
    inverse = 1.0 / total
    fin[0, 0:1, :] = top
    fin[0, 1:2, :] = inverse
    fin[0, 2:3, :] = moment * inverse

    def fin_send(r):
        return copy(fin.at[0], fin.at[r], fn_s.at[r], fn_r.at[r], dev(x, z + r, core))

    for r in (4, 3, 5, 2, 6, 1, 7):
        send(fin_send(r))

    def z_sum(d, i, what):
        return copy(
            zs.at[d, i, what], zr.at[d, i, what], za_s.at[d, i, what], za_r.at[d, i, what],
            z_right if d == 0 else z_left,
        )

    def z_part(r, what):
        scale = jnp.exp2((run[r, 0:1, :] - fin[r, 0:1, :]) * ALPHA) * fin[r, 1:2, :]
        if what == 0:
            return accv[r, 0:HD, :] * scale
        return (accw[r] - fin[r, 2:3, :] * accv[r, HD:, :]) * (scale * INV_ROOT)

    def z_add(i):
        for what in range(2):
            for d in range(2):
                r = 4 + i if d == 0 else 4 - i
                if i == 0 and what != d:
                    continue
                part = z_part(r, what)
                if i > 1 or (i == 1 and what == d):
                    z_sum(d, i - 1, what).wait_recv()
                    part = part + zr[d, i - 1, what].astype(F32)
                zs[d, i, what] = part.astype(BF16)
                send(z_sum(d, i, what))

    def sib_send(s):
        return copy(sbs.at[s], sbr.at[s], sb_s.at[s], sb_r.at[s], sib)

    mine = pl.ds(pl.multiple_of(core * T, T), T)
    other = pl.ds(pl.multiple_of((1 - core) * T, T), T)

    def key_part(s, u, r_low, r_high):
        kacc[s] = jnp.zeros((2 * HD, C), F32)

        def body(i, _):
            r = i % Z
            scale = jnp.exp2((pst[r, u, 0:1, :] - fin[r, 0:1, :]) * ALPHA) * fin[r, 1:2, :]
            root = scale * INV_ROOT
            shift = root * (pst[r, u, 1:2, :] - fin[r, 2:3, :])
            q = qt[r].astype(F32)
            left = jnp.concatenate(
                [(gt[r].astype(F32) * scale).astype(BF16), (q * shift).astype(BF16)], axis=0
            )
            sum_e = dot_nt(left, eb[r, u])
            sum_t = dot_nt((q * root).astype(BF16), tb[r, u])
            kacc[s, 0:HD, :] += sum_e[0:HD, :]
            kacc[s, HD:, :] += sum_e[HD:, :] + sum_t
            return 0

        lax.fori_loop(r_low, r_high, body, 0)
        sbs[s] = kacc[s, :, other].astype(BF16)
        send(sib_send(s))

    def own_part(s, what):
        rows = slice(what * HD, (what + 1) * HD)
        return kacc[s, rows, mine] + sbr[s, rows, :].astype(F32)

    x_target = [x_right, x_left, x_left, x_left, x_right, x_right]

    def x_sum(i):
        return copy(xs.at[i], xr.at[i], xr_s.at[i], xr_r.at[i], x_target[i])

    def x_send(i, part):
        xs[i] = part.astype(BF16)
        send(x_sum(i))

    for r in (4, 5, 3, 6, 2, 7, 1):
        fin_send(r).wait_recv()
        if r == 4:
            z_add(0)
    key_part(2, 2, 0, jnp.where(x >= 2, Z, 0))
    z_add(1)
    sib_send(2).wait_recv()
    x_send(0, own_part(2, 0))
    x_send(1, own_part(2, 1))
    key_part(1, 1, 0, jnp.where(x >= 1, Z, 0))
    z_add(2)
    sib_send(1).wait_recv()
    x_send(2, own_part(1, 0))
    key_part(3, 0, 4, jnp.where(x == X - 1, z + 1, 4))
    sib_send(3).wait_recv()
    x_send(5, own_part(3, 1))
    x_sum(1).wait_recv()
    x_send(3, own_part(1, 1) + xr[1].astype(F32))
    x_sum(0).wait_recv()
    x_send(4, own_part(3, 0) + xr[0].astype(F32))
    key_part(0, 0, z + 1, Z + 1)
    z_add(3)
    sib_send(0).wait_recv()
    for what, near in ((0, (2, 4)), (1, (3, 5))):
        part = own_part(0, what)
        for i in near:
            x_sum(i).wait_recv()
            part = part + xr[i].astype(F32)
        out_ref[3 - what] = part.T.astype(BF16)

    for what in range(2):
        part = z_part(0, what)
        for d in range(2):
            z_sum(d, 3, what).wait_recv()
            part = part + zr[d, 3, what].astype(F32)
        out_ref[what] = part.T.astype(BF16)

    for op in (*q_right, *q_left, *g_right, *g_left, *k_sib, *v_sib):
        op.wait_send()
    for op in (k_right, v_right, k_left, v_left, k_far, v_far, *started):
        op.wait_send()
    for r in range(1, Z):
        stat_send(r).wait_send()


def hand_on(all_ref, *outs):
    for i, out in enumerate(outs):
        out[...] = all_ref[i]


def per_device(queries, keys, values, out_grad, segments):
    vmem = pl.BlockSpec(memory_space=pltpu.VMEM)
    dma = pltpu.SemaphoreType.DMA
    sums = pl.pallas_call(
        kernel,
        out_shape=jax.ShapeDtypeStruct((4, T, HD), BF16),
        in_specs=[vmem] * 5,
        out_specs=vmem,
        scratch_shapes=[
            pltpu.VMEM((SEG_ROWS, HD), F32),
            pltpu.VMEM((Z, T + SEG_ROWS, HD), BF16),
            pltpu.VMEM((Z, T, HD), BF16),
            pltpu.VMEM((Z, HD, T), BF16),
            pltpu.VMEM((Z, HD, T), BF16),
            pltpu.VMEM((X, 2, T + SEG_ROWS, HD), BF16),
            pltpu.VMEM((X, 2, T, HD), BF16),
            pltpu.VMEM((X, 2 * HD, C), BF16),
            pltpu.VMEM((Z, 3, C, T), BF16),
            pltpu.VMEM((Z, 3, C, T), BF16),
            pltpu.VMEM((Z, 3, 8, T), F32),
            pltpu.VMEM((Z, 8, T), F32),
            pltpu.VMEM((Z, 2 * HD, T), F32),
            pltpu.VMEM((Z, HD, T), F32),
            pltpu.VMEM((X, 2 * HD, C), F32),
            pltpu.VMEM((X, 16, T), F32),
            pltpu.VMEM((Z, 8, T), F32),
            pltpu.VMEM((Z, 8, T), F32),
            pltpu.VMEM((2, 4, 2, HD, T), BF16),
            pltpu.VMEM((2, 4, 2, HD, T), BF16),
            pltpu.VMEM((X, 2 * HD, T), BF16),
            pltpu.VMEM((X, 2 * HD, T), BF16),
            pltpu.VMEM((6, HD, T), BF16),
            pltpu.VMEM((6, HD, T), BF16),
            dma((Z,)), dma((Z,)), dma((Z,)), dma((Z,)),
            dma((14,)), dma((14,)),
            dma((Z,)), dma((Z,)), dma((Z,)), dma((Z,)),
            dma((2, 4, 2)), dma((2, 4, 2)),
            dma((X,)), dma((X,)), dma((6,)), dma((6,)),
        ],
        compiler_params=pltpu.CompilerParams(
            collective_id=0, has_side_effects=True, vmem_limit_bytes=58 * 1024 * 1024
        ),
        cost_estimate=pl.CostEstimate(
            flops=4 * 10**9, bytes_accessed=600_000, transcendentals=2 * 10**6
        ),
    )(queries, keys, values, out_grad, segments.reshape(T // HD, HD))
    return pl.pallas_call(
        hand_on,
        out_shape=(jax.ShapeDtypeStruct((T, HD), BF16),) * 4,
        in_specs=[vmem],
        out_specs=(vmem,) * 4,
    )(sums)


def solution(mesh):
    rows = P(("dp", "ctx"), None)
    return jax.shard_map(
        per_device,
        mesh=mesh,
        in_specs=(rows, rows, rows, rows, P(("dp", "ctx"))),
        out_specs=(rows, rows, rows, rows),
        check_vma=False,
    )
```

```python
import functools
import math

import jax
import jax.numpy as jnp
from jax import lax
from jax.experimental import pallas as pl
from jax.experimental.pallas import tpu as pltpu
from jax.sharding import PartitionSpec as P

MESH = pl.DeviceIdType.MESH
HD = 128
X, Z = 4, 8
T = 256
C = 2 * T
SEG_ROWS = 16
NEG = -1e30
INV_ROOT = 1.0 / math.sqrt(HD)
ALPHA = INV_ROOT * math.log2(math.e)
F32 = jnp.float32
BF16 = jnp.bfloat16
NT = (((1,), (1,)), ((), ()))


def dot_nt(a, b):
    return lax.dot_general(a, b, NT, preferred_element_type=F32)


def dot(a, b):
    return jnp.dot(a, b, preferred_element_type=F32)


def kernel(
    q_ref, k_ref, v_ref, g_ref, seg_ref, out_ref,
    segf, qs, gs, qt, gt, ks, vs, vkt, eb, tb, sbuf, dbuf, pst, run, accv, accw,
    left_e, left_t, kacc, cnt, sto, sti, fin, zs, zr, sbs, sbr, xs, xr,
    zq_s, zq_r, zg_s, zg_r, kv_s, kv_r, st_s, st_r, fn_s, fn_r,
    za_s, za_r, sb_s, sb_r, xr_s, xr_r,
):
    ctx = lax.axis_index("ctx")
    x = ctx // (2 * Z)
    z = (ctx // 2) % Z
    core = ctx % 2

    def dev(xx, zz, cc):
        return {"ctx": ((xx + X) % X) * (2 * Z) + ((zz + Z) % Z) * 2 + cc}

    sib = dev(x, z, 1 - core)
    z_right, z_left = dev(x, z + 1, core), dev(x, z - 1, core)
    x_right, x_left = dev(x + 1, z, core), dev(x - 1, z, core)

    barrier = pltpu.get_barrier_semaphore()
    for peer in (z_right, z_left, x_right, x_left, sib):
        pl.semaphore_signal(barrier, inc=1, device_id=peer, device_id_type=MESH)

    segf[...] = jnp.zeros_like(segf)
    segf[0 : T // HD, :] = seg_ref[...].astype(F32)
    seg_rows = segf[...].astype(BF16)
    qs[0, 0:T, :] = q_ref[...]
    qs[0, T : T + SEG_ROWS, :] = seg_rows
    gs[0] = g_ref[...]
    ks[0, core, 0:T, :] = k_ref[...]
    ks[0, core, T : T + SEG_ROWS, :] = seg_rows
    vs[0, core] = v_ref[...]

    pl.semaphore_wait(barrier, 5)

    def copy(src, dst, send, recv, target):
        return pltpu.make_async_remote_copy(
            src_ref=src, dst_ref=dst, send_sem=send, recv_sem=recv,
            device_id=target, device_id_type=MESH,
        )

    started = []

    def send(op):
        op.start()
        started.append(op)

    half = (slice(0, HD), slice(HD, T + SEG_ROWS))

    def q_hop(src, dst, target, h):
        return copy(
            qs.at[src, half[h], :], qs.at[dst, half[h], :], zq_s.at[dst, h], zq_r.at[dst, h], target
        )

    def g_hop(src, dst, target, h):
        rows = slice(h * HD, (h + 1) * HD)
        return copy(gs.at[src, rows, :], gs.at[dst, rows, :], zg_s.at[dst, h], zg_r.at[dst, h], target)

    def k_hop(i, src, dst, target):
        return copy(ks.at[src, core], ks.at[dst, core], kv_s.at[i], kv_r.at[i], target)

    def v_hop(i, src, dst, target):
        return copy(vs.at[src, core], vs.at[dst, core], kv_s.at[i], kv_r.at[i], target)

    q_right = [[q_hop(j, j + 1, z_right, h) for h in range(2)] for j in range(4)]
    q_left = [[q_hop((8 - j) % 8, 7 - j, z_left, h) for h in range(2)] for j in range(3)]
    g_right = [[g_hop(j, j + 1, z_right, h) for h in range(2)] for j in range(3)]
    g_left = [[g_hop((8 - j) % 8, 7 - j, z_left, h) for h in range(2)] for j in range(4)]
    k_sib = [k_hop(s, s, s, sib) for s in range(4)]
    v_sib = [v_hop(4 + s, s, s, sib) for s in range(4)]
    k_right, v_right = k_hop(8, 0, 1, x_right), v_hop(9, 0, 1, x_right)
    k_left, v_left = k_hop(10, 0, 3, x_left), v_hop(11, 0, 3, x_left)
    k_far, v_far = k_hop(12, 1, 2, x_right), v_hop(13, 3, 2, x_left)

    for op in (
        q_right[0][0], q_left[0][0], k_right, k_left, k_sib[0], v_sib[0],
        q_right[0][1], q_left[0][1], v_left, v_right,
        g_right[0][0], g_left[0][0], g_right[0][1], g_left[0][1],
    ):
        op.start()

    def z_step(j):
        for right, left in ((q_right, q_left), (g_right, g_left)):
            for h in range(2):
                for hops in (right, left):
                    if j <= len(hops):
                        hops[j - 1][h].wait_recv()
                    if j < len(hops):
                        hops[j][h].start()

    doc16 = lax.broadcasted_iota(jnp.int32, (16, HD), 0).astype(F32)

    def prepare_keys(s):
        below = jnp.zeros((16, HD), F32)
        for c in range(2):
            lanes = slice(s * C + c * T, s * C + (c + 1) * T)
            vkt[0:HD, lanes] = vs[s, c].T
            vkt[HD:, lanes] = ks[s, c, 0:T, :].T
            seg = ks[s, c, T : T + SEG_ROWS, :].astype(F32)
            for h in range(T // HD):
                below += jnp.where(seg[h : h + 1, :] < doc16, 1.0, 0.0)
        cnt[s] = jnp.broadcast_to(jnp.sum(below, axis=1, keepdims=True), (16, T))

    def prepare_queries(r):
        qt[r] = qs[r, 0:T, :].T
        gt[r] = gs[r].T

    key_row = lax.broadcasted_iota(jnp.int32, (T, T), 0).astype(F32)
    query_lane = lax.broadcasted_iota(jnp.int32, (1, T), 1).astype(F32)
    doc_q = lax.broadcasted_iota(jnp.int32, (16, T), 0).astype(F32)

    def near_slot(r):
        own = (r == 0) | (r > z)
        used = own | ((x == X - 1) & (r >= 4))
        return used, jnp.where(own, 0, 3)

    def block_lanes(r):
        return pl.ds(pl.multiple_of(r * T, T), T)

    def piece(r, which, chunks, diagonal=False):
        seg = qs[r, T : T + SEG_ROWS, :].astype(F32)
        seg_q = jnp.concatenate([seg[0:1, :], seg[1:2, :]], axis=1)
        same = seg_q == doc_q
        q = qs[r, 0:T, :]
        g = gs[r]
        lanes = block_lanes(r)
        blocks = []
        top = jnp.full((1, T), NEG, F32)
        for u, s in chunks:
            low = jnp.sum(jnp.where(same, cnt[s], 0.0), axis=0, keepdims=True)
            if u == 2:
                low = jnp.where(x >= 2, low, 1e9)
            for c in range(2):
                b = len(blocks)
                sc = dot_nt(ks[s, c, 0:T, :], q)
                allowed = key_row >= low - c * T
                if diagonal:
                    allowed = allowed & (key_row <= query_lane + ((core - c) * T).astype(F32))
                sc = jnp.where(allowed, sc, NEG)
                sbuf[b] = sc
                top = jnp.maximum(top, jnp.max(sc, axis=0, keepdims=True))
                blocks.append((s, c, slice(u * C + c * T, u * C + (c + 1) * T)))
        total = jnp.zeros((1, T), F32)
        moment = jnp.zeros((1, T), F32)
        for b, (s, c, rows) in enumerate(blocks):
            e = jnp.exp2((sbuf[b] - top) * ALPHA)
            weighted = e * dot_nt(vs[s, c], g)
            eb[rows, lanes] = e.astype(BF16)
            sbuf[b] = e
            dbuf[b] = weighted
            total += jnp.sum(e, axis=0, keepdims=True)
            moment += jnp.sum(weighted, axis=0, keepdims=True)
        mean = moment / total
        for b, (s, c, rows) in enumerate(blocks):
            tb[rows, lanes] = (dbuf[b] - sbuf[b] * mean).astype(BF16)
        pst[r, which, 0:1, :] = top
        pst[r, which, 1:2, :] = mean
        old = run[r, 0:1, :]
        new = jnp.maximum(old, top)
        keep = jnp.exp2((old - new) * ALPHA)
        add = jnp.exp2((top - new) * ALPHA)
        run[r, 0:1, :] = new
        run[r, 1:2, :] = run[r, 1:2, :] * keep + total * add
        run[r, 2:3, :] = run[r, 2:3, :] * keep + moment * add

    def near_piece(r):
        used, s = near_slot(r)

        @pl.when(used)
        def _():
            piece(r, 0, [(0, s)])

    def products(r):
        lanes = block_lanes(r)

        def add_part(which, rows, keys):
            add = jnp.exp2((pst[r, which, 0:1, :] - run[r, 0:1, :]) * ALPHA)
            part_v = dot(vkt[:, keys], eb[rows, lanes])
            part_t = dot(vkt[HD:, keys], tb[rows, lanes])
            accv[r] += part_v * add
            accw[r] += (part_t + pst[r, which, 1:2, :] * part_v[HD:, :]) * add

        accv[r] = jnp.zeros((2 * HD, T), F32)
        accw[r] = jnp.zeros((HD, T), F32)
        used, s = near_slot(r)

        @pl.when(used)
        def _():
            add_part(0, slice(0, C), pl.ds(pl.multiple_of(s * C, C), C))

        @pl.when(x >= 1)
        def _():
            add_part(1, slice(C, 3 * C), slice(C, 3 * C))

    for r in range(Z):
        run[r, 0:1, :] = jnp.full((1, T), NEG, F32)
        run[r, 1:8, :] = jnp.zeros((7, T), F32)

    def pack(i, values):
        for n in range(3):
            for h in range(2):
                sto[i, 2 * n + h : 2 * n + h + 1, :] = values[n][:, h * HD : (h + 1) * HD]

    def merge(parts):
        top = functools.reduce(jnp.maximum, [p[0:2, :] for p in parts])
        scales = [jnp.exp2((p[0:2, :] - top) * ALPHA) for p in parts]
        total = sum(p[2:4, :] * scale for p, scale in zip(parts, scales))
        moment = sum(p[4:6, :] * scale for p, scale in zip(parts, scales))
        return top, total, moment

    def stat_send(r):
        return copy(sto.at[r], sti.at[32 + r], st_s.at[r], st_r.at[r], dev(x, z - r, core))

    far_blocks = (3, 5, 4)

    def total_send(kind, d):
        r = 0 if kind == 0 else far_blocks[kind - 1]
        slot = kind * Z + (d + r) % Z
        return copy(sto.at[r], sti.at[slot], fn_s.at[0], fn_r.at[0], dev(x, z + d, core))

    prepare_queries(0)
    k_sib[0].wait_recv()
    v_sib[0].wait_recv()
    prepare_keys(0)
    piece(0, 0, [(0, 0)], diagonal=True)

    k_right.wait_recv()
    k_far.start()
    k_sib[1].start()
    for h in range(2):
        q_right[0][h].wait_recv()
        q_right[1][h].start()
        q_left[0][h].wait_recv()
        q_left[1][h].start()
    k_left.wait_recv()
    k_sib[3].start()
    v_left.wait_recv()
    v_far.start()
    v_sib[3].start()
    v_right.wait_recv()
    v_sib[1].start()
    for h in range(2):
        g_right[0][h].wait_recv()
        g_right[1][h].start()
        g_left[0][h].wait_recv()
        g_left[1][h].start()
    prepare_queries(1)
    prepare_queries(7)
    for s in (1, 3):
        k_sib[s].wait_recv()
        v_sib[s].wait_recv()
        prepare_keys(s)
    k_far.wait_recv()
    k_sib[2].start()

    def early(i, _):
        near_piece(jnp.where(i == 0, 1, 7))
        return 0

    lax.fori_loop(0, 2, early, 0)
    z_step(2)
    v_far.wait_recv()
    v_sib[2].start()
    prepare_queries(2)
    prepare_queries(6)
    k_sib[2].wait_recv()
    v_sib[2].wait_recv()
    prepare_keys(2)

    def block(i, _):
        @pl.when(i == 3)
        def _():
            z_step(3)

        @pl.when(i == 5)
        def _():
            prepare_queries(3)
            prepare_queries(5)

        @pl.when(i == 7)
        def _():
            z_step(4)
            for r in (1, 7, 2, 6):
                stat_send(r).wait_recv()
            own = [run[0, n : n + 1, :] for n in range(3)]
            pack(0, own)
            merged = merge([sto[0]] + [sti[32 + r] for r in (1, 7, 2, 6)])
            for n in range(3):
                sto[0, 2 * n : 2 * n + 2, :] = merged[n]
            for d in (4, 3, 5, 2, 6, 1, 7):
                total_send(0, d).start()
            prepare_queries(4)

        r = jnp.where(i % 2 == 1, (i + 1) // 2, (8 - i // 2) % 8)

        @pl.when(i >= 3)
        def _():
            near_piece(r)

        @pl.when(x >= 1)
        def _():
            piece(r, 1, [(1, 1), (2, 2)])

        @pl.when(i > 0)
        def _():
            pack(r, [run[r, n : n + 1, :] for n in range(3)])

        @pl.when((i > 0) & (i < 5))
        def _():
            stat_send(r).start()

        return 0

    lax.fori_loop(0, Z, block, 0)
    for kind in (3, 1, 2):
        for d in (4, 3, 5, 2, 6, 1, 7):
            total_send(kind, d).start()

    def all_products(i, _):
        products((i + 4) % Z)
        return 0

    lax.fori_loop(0, Z, all_products, 0)

    pltpu.make_async_copy(
        sti.at[pl.ds(0, 4 * (Z - 1))], sti.at[pl.ds(0, 4 * (Z - 1))], fn_r.at[0]
    ).wait()
    for r in range(Z):
        parts = [sto[0] if r == 0 else sti[r]]
        for kind in (1, 2, 3):
            parts.append(sto[r] if far_blocks[kind - 1] == r else sti[kind * Z + r])
        top, total, moment = merge(parts)
        inverse = 1.0 / total
        for n, value in enumerate((top, inverse, moment * inverse)):
            fin[r, n : n + 1, :] = jnp.concatenate([value[0:1, :], value[1:2, :]], axis=1)

    def z_sum(d, i, what, h):
        return copy(
            zs.at[d, i, what, h], zr.at[d, i, what, h], za_s.at[d, i, what, h], za_r.at[d, i, what, h],
            z_right if d == 0 else z_left,
        )

    def z_part(r, what, h):
        rows = slice(h * 64, (h + 1) * 64)
        later = slice(HD + h * 64, HD + (h + 1) * 64)
        scale = jnp.exp2((run[r, 0:1, :] - fin[r, 0:1, :]) * ALPHA) * fin[r, 1:2, :]
        if what == 0:
            return accv[r, rows, :] * scale
        return (accw[r, rows, :] - fin[r, 2:3, :] * accv[r, later, :]) * (scale * INV_ROOT)

    def z_add(i):
        for what in range(2):
            for h in range(2):
                for d in range(2):
                    r = 4 + i if d == 0 else 4 - i
                    if i == 0 and what != d:
                        continue
                    part = z_part(r, what, h)
                    if i > 1 or (i == 1 and what == d):
                        z_sum(d, i - 1, what, h).wait_recv()
                        part = part + zr[d, i - 1, what, h].astype(F32)
                    zs[d, i, what, h] = part.astype(BF16)
                    send(z_sum(d, i, what, h))

    def sib_send(s):
        return copy(sbs.at[s], sbr.at[s], sb_s.at[s], sb_r.at[s], sib)

    mine = pl.ds(pl.multiple_of(core * T, T), T)
    other = pl.ds(pl.multiple_of((1 - core) * T, T), T)

    def factors(r, which):
        scale = jnp.exp2((pst[r, which, 0:1, :] - fin[r, 0:1, :]) * ALPHA) * fin[r, 1:2, :]
        root = scale * INV_ROOT
        shift = root * (pst[r, which, 1:2, :] - fin[r, 2:3, :])
        q = qt[r].astype(F32)
        return (
            (gt[r].astype(F32) * scale).astype(BF16),
            (q * shift).astype(BF16),
            (q * root).astype(BF16),
        )

    def sib_half(s):
        sbs[s] = kacc[s, :, other].astype(BF16)
        send(sib_send(s))

    def far_key(s):
        kacc[s] = jnp.zeros((2 * HD, C), F32)

        @pl.when(x >= s)
        def _():
            rows = slice(s * C, (s + 1) * C)
            kacc[s] = dot_nt(left_e[...], eb[rows, :])
            kacc[s, HD:, :] += dot_nt(left_t[...], tb[rows, :])

        sib_half(s)

    def near_key(s, r_low, r_high):
        kacc[s] = jnp.zeros((2 * HD, C), F32)

        def body(i, _):
            r = i % Z
            lanes = block_lanes(r)
            g_scaled, q_shift, q_root = factors(r, 0)
            sum_e = dot_nt(jnp.concatenate([g_scaled, q_shift], axis=0), eb[0:C, lanes])
            sum_t = dot_nt(q_root, tb[0:C, lanes])
            kacc[s, 0:HD, :] += sum_e[0:HD, :]
            kacc[s, HD:, :] += sum_e[HD:, :] + sum_t
            return 0

        lax.fori_loop(r_low, r_high, body, 0)
        sib_half(s)

    def own_part(s, what):
        rows = slice(what * HD, (what + 1) * HD)
        return kacc[s, rows, mine] + sbr[s, rows, :].astype(F32)

    x_target = [x_right, x_left, x_left, x_left, x_right, x_right]

    def x_sum(i):
        return copy(xs.at[i], xr.at[i], xr_s.at[i], xr_r.at[i], x_target[i])

    def x_send(i, part):
        xs[i] = part.astype(BF16)
        send(x_sum(i))

    z_add(0)

    @pl.when(x >= 1)
    def _():
        def scale_left(r, _):
            lanes = block_lanes(r)
            left_e[0:HD, lanes], left_e[HD:, lanes], left_t[:, lanes] = factors(r, 1)
            return 0

        lax.fori_loop(0, Z, scale_left, 0)

    far_key(2)
    far_key(1)
    sib_send(2).wait_recv()
    x_send(0, own_part(2, 0))
    x_send(1, own_part(2, 1))
    z_add(1)
    near_key(3, 4, jnp.where(x == X - 1, z + 1, 4))
    sib_send(1).wait_recv()
    x_send(2, own_part(1, 0))
    sib_send(3).wait_recv()
    x_send(5, own_part(3, 1))
    z_add(2)
    near_key(0, z + 1, Z + 1)
    x_sum(1).wait_recv()
    x_send(3, own_part(1, 1) + xr[1].astype(F32))
    x_sum(0).wait_recv()
    x_send(4, own_part(3, 0) + xr[0].astype(F32))
    z_add(3)
    sib_send(0).wait_recv()
    for what, near in ((0, (2, 4)), (1, (3, 5))):
        part = own_part(0, what)
        for i in near:
            x_sum(i).wait_recv()
            part = part + xr[i].astype(F32)
        out_ref[3 - what] = part.T.astype(BF16)

    for what in range(2):
        halves = []
        for h in range(2):
            part = z_part(0, what, h)
            for d in range(2):
                z_sum(d, 3, what, h).wait_recv()
                part = part + zr[d, 3, what, h].astype(F32)
            halves.append(part)
        out_ref[what] = jnp.concatenate(halves, axis=0).T.astype(BF16)

    for hops in (*q_right, *q_left, *g_right, *g_left):
        for op in hops:
            op.wait_send()
    for op in (*k_sib, *v_sib, k_right, v_right, k_left, v_left, k_far, v_far, *started):
        op.wait_send()
    for r in (1, 7, 2, 6):
        stat_send(r).wait_send()
    pltpu.make_async_copy(
        sti.at[pl.ds(0, 4 * (Z - 1))], sti.at[pl.ds(0, 4 * (Z - 1))], fn_s.at[0]
    ).wait()


def hand_on(all_ref, *outs):
    for i, out in enumerate(outs):
        out[...] = all_ref[i]


def per_device(queries, keys, values, out_grad, segments):
    vmem = pl.BlockSpec(memory_space=pltpu.VMEM)
    dma = pltpu.SemaphoreType.DMA
    sums = pl.pallas_call(
        kernel,
        out_shape=jax.ShapeDtypeStruct((4, T, HD), BF16),
        in_specs=[vmem] * 5,
        out_specs=vmem,
        scratch_shapes=[
            pltpu.VMEM((SEG_ROWS, HD), F32),
            pltpu.VMEM((Z, T + SEG_ROWS, HD), BF16),
            pltpu.VMEM((Z, T, HD), BF16),
            pltpu.VMEM((Z, HD, T), BF16),
            pltpu.VMEM((Z, HD, T), BF16),
            pltpu.VMEM((X, 2, T + SEG_ROWS, HD), BF16),
            pltpu.VMEM((X, 2, T, HD), BF16),
            pltpu.VMEM((2 * HD, X * C), BF16),
            pltpu.VMEM((3 * C, Z * T), BF16),
            pltpu.VMEM((3 * C, Z * T), BF16),
            pltpu.VMEM((4, T, T), F32),
            pltpu.VMEM((4, T, T), F32),
            pltpu.VMEM((Z, 2, 8, T), F32),
            pltpu.VMEM((Z, 8, T), F32),
            pltpu.VMEM((Z, 2 * HD, T), F32),
            pltpu.VMEM((Z, HD, T), F32),
            pltpu.VMEM((2 * HD, Z * T), BF16),
            pltpu.VMEM((HD, Z * T), BF16),
            pltpu.VMEM((X, 2 * HD, C), F32),
            pltpu.VMEM((X, 16, T), F32),
            pltpu.VMEM((Z, 8, HD), F32),
            pltpu.VMEM((5 * Z, 8, HD), F32),
            pltpu.VMEM((Z, 8, T), F32),
            pltpu.VMEM((2, 4, 2, 2, HD // 2, T), BF16),
            pltpu.VMEM((2, 4, 2, 2, HD // 2, T), BF16),
            pltpu.VMEM((X, 2 * HD, T), BF16),
            pltpu.VMEM((X, 2 * HD, T), BF16),
            pltpu.VMEM((6, HD, T), BF16),
            pltpu.VMEM((6, HD, T), BF16),
            dma((Z, 2)), dma((Z, 2)), dma((Z, 2)), dma((Z, 2)),
            dma((14,)), dma((14,)),
            dma((Z,)), dma((Z,)), dma((1,)), dma((1,)),
            dma((2, 4, 2, 2)), dma((2, 4, 2, 2)),
            dma((X,)), dma((X,)), dma((6,)), dma((6,)),
        ],
        compiler_params=pltpu.CompilerParams(
            collective_id=0, has_side_effects=True, vmem_limit_bytes=44 * 1024 * 1024
        ),
        cost_estimate=pl.CostEstimate(
            flops=4 * 10**9, bytes_accessed=600_000, transcendentals=2 * 10**6
        ),
    )(queries, keys, values, out_grad, segments.reshape(T // HD, HD))
    return pl.pallas_call(
        hand_on,
        out_shape=(jax.ShapeDtypeStruct((T, HD), BF16),) * 4,
        in_specs=[vmem],
        out_specs=(vmem,) * 4,
    )(sums)


def solution(mesh):
    rows = P(("dp", "ctx"), None)
    return jax.shard_map(
        per_device,
        mesh=mesh,
        in_specs=(rows, rows, rows, rows, P(("dp", "ctx"))),
        out_specs=(rows, rows, rows, rows),
        check_vma=False,
    )
```

```python
import functools
import math

import jax
import jax.numpy as jnp
from jax import lax
from jax.experimental import pallas as pl
from jax.experimental.pallas import tpu as pltpu
from jax.sharding import PartitionSpec as P

MESH = pl.DeviceIdType.MESH
HD = 128
X, Z = 4, 8
T = 256
C = 2 * T
SEG_ROWS = 16
NEG = -1e30
INV_ROOT = 1.0 / math.sqrt(HD)
ALPHA = INV_ROOT * math.log2(math.e)
F32 = jnp.float32
BF16 = jnp.bfloat16
NT = (((1,), (1,)), ((), ()))


def dot_nt(a, b):
    return lax.dot_general(a, b, NT, preferred_element_type=F32)


def dot(a, b):
    return jnp.dot(a, b, preferred_element_type=F32)


def pick(index, values):
    result = values[-1]
    for i in range(len(values) - 2, -1, -1):
        result = jnp.where(index == i, values[i], result)
    return result


def kernel(
    q_ref, k_ref, v_ref, g_ref, seg_ref, out_ref,
    segi, segf, out_v, qs, gs, qt, gt, ks, vs, vkt, eb, tb, sbuf, dbuf, pst, run, accv, accw,
    left_e, left_t, kacc, cnt, sto, sti, fin, zs, zr, sbs, sbr, xs, xr,
    zq_s, zq_r, zg_s, zg_r, kv_s, kv_r, st_s, st_r, fn_s, fn_r,
    za_s, za_r, sb_s, sb_r, xr_s, xr_r, in_s, out_s,
):
    ctx = lax.axis_index("ctx")
    x = ctx // (2 * Z)
    z = (ctx // 2) % Z
    core = ctx % 2

    def dev(xx, zz, cc):
        return {"ctx": ((xx + X) % X) * (2 * Z) + ((zz + Z) % Z) * 2 + cc}

    sib = dev(x, z, 1 - core)
    z_right, z_left = dev(x, z + 1, core), dev(x, z - 1, core)
    x_right, x_left = dev(x + 1, z, core), dev(x - 1, z, core)

    barrier = pltpu.get_barrier_semaphore()
    for peer in (z_right, z_left, x_right, x_left, sib):
        pl.semaphore_signal(barrier, inc=1, device_id=peer, device_id_type=MESH)

    loads = [
        pltpu.make_async_copy(src, dst, in_s.at[i])
        for i, (src, dst) in enumerate((
            (seg_ref, segi),
            (q_ref, qs.at[0, 0:T, :]),
            (k_ref, ks.at[0, core, 0:T, :]),
            (v_ref, vs.at[0, core]),
            (g_ref, gs.at[0]),
        ))
    ]
    for op in loads:
        op.start()
    segf[...] = jnp.zeros_like(segf)
    for r in range(Z):
        run[r, 0:1, :] = jnp.full((1, T), NEG, F32)
        run[r, 1:8, :] = jnp.zeros((7, T), F32)
    loads[0].wait()
    segf[0 : T // HD, :] = segi[...].astype(F32)
    seg_rows = segf[...].astype(BF16)
    qs[0, T : T + SEG_ROWS, :] = seg_rows
    ks[0, core, T : T + SEG_ROWS, :] = seg_rows
    for op in loads[1:]:
        op.wait()

    pl.semaphore_wait(barrier, 5)

    def copy(src, dst, send, recv, target):
        return pltpu.make_async_remote_copy(
            src_ref=src, dst_ref=dst, send_sem=send, recv_sem=recv,
            device_id=target, device_id_type=MESH,
        )

    started = []

    def send(op):
        op.start()
        started.append(op)

    half = (slice(0, HD), slice(HD, T + SEG_ROWS))

    def q_hop(src, dst, target, h):
        return copy(
            qs.at[src, half[h], :], qs.at[dst, half[h], :], zq_s.at[dst, h], zq_r.at[dst, h], target
        )

    def g_hop(src, dst, target, h):
        rows = slice(h * HD, (h + 1) * HD)
        return copy(gs.at[src, rows, :], gs.at[dst, rows, :], zg_s.at[dst, h], zg_r.at[dst, h], target)

    def k_hop(i, src, dst, target):
        return copy(ks.at[src, core], ks.at[dst, core], kv_s.at[i], kv_r.at[i], target)

    def v_hop(i, src, dst, target):
        return copy(vs.at[src, core], vs.at[dst, core], kv_s.at[i], kv_r.at[i], target)

    q_right = [[q_hop(j, j + 1, z_right, h) for h in range(2)] for j in range(4)]
    q_left = [[q_hop((8 - j) % 8, 7 - j, z_left, h) for h in range(2)] for j in range(3)]
    g_right = [[g_hop(j, j + 1, z_right, h) for h in range(2)] for j in range(3)]
    g_left = [[g_hop((8 - j) % 8, 7 - j, z_left, h) for h in range(2)] for j in range(4)]
    k_sib = [k_hop(s, s, s, sib) for s in range(4)]
    v_sib = [v_hop(4 + s, s, s, sib) for s in range(4)]
    k_right, v_right = k_hop(8, 0, 1, x_right), v_hop(9, 0, 1, x_right)
    k_left, v_left = k_hop(10, 0, 3, x_left), v_hop(11, 0, 3, x_left)
    k_far, v_far = k_hop(12, 1, 2, x_right), v_hop(13, 3, 2, x_left)

    for op in (
        q_right[0][0], q_left[0][0], k_right, v_left, k_sib[0], v_sib[0],
        q_right[0][1], q_left[0][1], v_right, k_left,
        g_right[0][0], g_left[0][0], g_right[0][1], g_left[0][1],
    ):
        op.start()

    def z_step(j, what):
        for h in range(2):
            for hops in ((q_right, q_left), (g_right, g_left))[what]:
                if j <= len(hops):
                    hops[j - 1][h].wait_recv()
                if j < len(hops):
                    hops[j][h].start()

    doc16 = lax.broadcasted_iota(jnp.int32, (16, HD), 0).astype(F32)

    def prepare_keys(s):
        below = jnp.zeros((16, HD), F32)
        for c in range(2):
            lanes = slice(s * C + c * T, s * C + (c + 1) * T)
            vkt[0:HD, lanes] = vs[s, c].T
            vkt[HD:, lanes] = ks[s, c, 0:T, :].T
            seg = ks[s, c, T : T + SEG_ROWS, :].astype(F32)
            for h in range(T // HD):
                below += jnp.where(seg[h : h + 1, :] < doc16, 1.0, 0.0)
        cnt[s] = jnp.broadcast_to(jnp.sum(below, axis=1, keepdims=True), (16, T))

    def prepare_queries(r):
        qt[r] = qs[r, 0:T, :].T
        gt[r] = gs[r].T

    key_row = lax.broadcasted_iota(jnp.int32, (T, T), 0).astype(F32)
    query_lane = lax.broadcasted_iota(jnp.int32, (1, T), 1).astype(F32)
    doc_q = lax.broadcasted_iota(jnp.int32, (16, T), 0).astype(F32)

    def near_slot(r):
        own = (r == 0) | (r > z)
        used = own | ((x == X - 1) & (r >= 4))
        return used, jnp.where(own, 0, 3)

    def block_lanes(r):
        return pl.ds(pl.multiple_of(r * T, T), T)

    def piece(r, which, chunks, diagonal=False):
        seg = qs[r, T : T + SEG_ROWS, :].astype(F32)
        seg_q = jnp.concatenate([seg[0:1, :], seg[1:2, :]], axis=1)
        same = seg_q == doc_q
        q = qs[r, 0:T, :]
        g = gs[r]
        lanes = block_lanes(r)
        blocks = []
        top = jnp.full((1, T), NEG, F32)
        for u, s in chunks:
            low = jnp.sum(jnp.where(same, cnt[s], 0.0), axis=0, keepdims=True)
            if u == 2:
                low = jnp.where(x >= 2, low, 1e9)
            for c in range(2):
                b = len(blocks)
                sc = dot_nt(ks[s, c, 0:T, :], q)
                allowed = key_row >= low - c * T
                if diagonal:
                    allowed = allowed & (key_row <= query_lane + ((core - c) * T).astype(F32))
                sc = jnp.where(allowed, sc, NEG)
                sbuf[b] = sc
                top = jnp.maximum(top, jnp.max(sc, axis=0, keepdims=True))
                blocks.append((s, c, slice(u * C + c * T, u * C + (c + 1) * T)))
        total = jnp.zeros((1, T), F32)
        moment = jnp.zeros((1, T), F32)
        for b, (s, c, rows) in enumerate(blocks):
            e = jnp.exp2((sbuf[b] - top) * ALPHA)
            weighted = e * dot_nt(vs[s, c], g)
            eb[rows, lanes] = e.astype(BF16)
            sbuf[b] = e
            dbuf[b] = weighted
            total += jnp.sum(e, axis=0, keepdims=True)
            moment += jnp.sum(weighted, axis=0, keepdims=True)
        mean = moment / total
        for b, (s, c, rows) in enumerate(blocks):
            tb[rows, lanes] = (dbuf[b] - sbuf[b] * mean).astype(BF16)
        pst[r, which, 0:1, :] = top
        pst[r, which, 1:2, :] = mean
        old = run[r, 0:1, :]
        new = jnp.maximum(old, top)
        keep = jnp.exp2((old - new) * ALPHA)
        add = jnp.exp2((top - new) * ALPHA)
        run[r, 0:1, :] = new
        run[r, 1:2, :] = run[r, 1:2, :] * keep + total * add
        run[r, 2:3, :] = run[r, 2:3, :] * keep + moment * add

    def near_piece(r):
        used, s = near_slot(r)

        @pl.when(used)
        def _():
            piece(r, 0, [(0, s)])

    def products(r):
        lanes = block_lanes(r)

        def add_part(which, rows, keys):
            add = jnp.exp2((pst[r, which, 0:1, :] - run[r, 0:1, :]) * ALPHA)
            part_v = dot(vkt[:, keys], eb[rows, lanes])
            part_t = dot(vkt[HD:, keys], tb[rows, lanes])
            accv[r] += part_v * add
            accw[r] += (part_t + pst[r, which, 1:2, :] * part_v[HD:, :]) * add

        accv[r] = jnp.zeros((2 * HD, T), F32)
        accw[r] = jnp.zeros((HD, T), F32)
        used, s = near_slot(r)

        @pl.when(used)
        def _():
            add_part(0, slice(0, C), pl.ds(pl.multiple_of(s * C, C), C))

        @pl.when(x >= 1)
        def _():
            add_part(1, slice(C, 3 * C), slice(C, 3 * C))

    def pack(i, values):
        for n in range(3):
            for h in range(2):
                sto[i, 2 * n + h : 2 * n + h + 1, :] = values[n][:, h * HD : (h + 1) * HD]

    def merge(parts):
        top = functools.reduce(jnp.maximum, [p[0:2, :] for p in parts])
        scales = [jnp.exp2((p[0:2, :] - top) * ALPHA) for p in parts]
        total = sum(p[2:4, :] * scale for p, scale in zip(parts, scales))
        moment = sum(p[4:6, :] * scale for p, scale in zip(parts, scales))
        return top, total, moment

    def stat_send(r):
        return copy(sto.at[r], sti.at[32 + r], st_s.at[r], st_r.at[r], dev(x, z - r, core))

    far_blocks = (3, 5, 4)

    def total_send(kind, d):
        r = 0 if kind == 0 else far_blocks[kind - 1]
        slot = kind * Z + (d + r) % Z
        return copy(sto.at[r], sti.at[slot], fn_s.at[0], fn_r.at[0], dev(x, z + d, core))

    prepare_queries(0)
    k_sib[0].wait_recv()
    v_sib[0].wait_recv()
    prepare_keys(0)
    piece(0, 0, [(0, 0)], diagonal=True)

    z_step(1, 0)
    k_right.wait_recv()
    k_far.start()
    k_sib[1].start()
    v_left.wait_recv()
    v_far.start()
    v_sib[3].start()
    z_step(1, 1)
    v_right.wait_recv()
    v_sib[1].start()
    k_left.wait_recv()
    k_sib[3].start()
    prepare_queries(1)
    prepare_queries(7)
    z_step(2, 0)
    for s in (1, 3):
        k_sib[s].wait_recv()
        v_sib[s].wait_recv()
        prepare_keys(s)
    k_far.wait_recv()
    k_sib[2].start()
    v_far.wait_recv()
    v_sib[2].start()

    def early(i, _):
        @pl.when(i == 1)
        def _():
            z_step(2, 1)
            prepare_queries(2)
            prepare_queries(6)

        near_piece(pick(i, [1, 7, 2, 6]))
        return 0

    lax.fori_loop(0, 4, early, 0)
    k_sib[2].wait_recv()
    v_sib[2].wait_recv()
    prepare_keys(2)

    def block(i, _):
        @pl.when(i == 1)
        def _():
            z_step(3, 0)

        @pl.when(i == 3)
        def _():
            z_step(3, 1)
            prepare_queries(3)
            prepare_queries(5)

        @pl.when(i == 7)
        def _():
            z_step(4, 0)
            z_step(4, 1)
            for r in (1, 7, 2, 6):
                stat_send(r).wait_recv()
            own = [run[0, n : n + 1, :] for n in range(3)]
            pack(0, own)
            merged = merge([sto[0]] + [sti[32 + r] for r in (1, 7, 2, 6)])
            for n in range(3):
                sto[0, 2 * n : 2 * n + 2, :] = merged[n]
            for kind in (1, 2, 0):
                for d in (4, 3, 5, 2, 6, 1, 7):
                    total_send(kind, d).start()
            prepare_queries(4)

        r = jnp.where(i % 2 == 1, (i + 1) // 2, (8 - i // 2) % 8)

        @pl.when(i >= 5)
        def _():
            near_piece(r)

        @pl.when(x >= 1)
        def _():
            piece(r, 1, [(1, 1), (2, 2)])

        @pl.when(i > 0)
        def _():
            pack(r, [run[r, n : n + 1, :] for n in range(3)])

        @pl.when((i > 0) & (i < 5))
        def _():
            stat_send(r).start()

        return 0

    lax.fori_loop(0, Z, block, 0)
    for d in (4, 3, 5, 2, 6, 1, 7):
        total_send(3, d).start()

    def all_products(i, _):
        products((i + 4) % Z)
        return 0

    lax.fori_loop(0, Z, all_products, 0)

    pltpu.make_async_copy(
        sti.at[pl.ds(0, 4 * (Z - 1))], sti.at[pl.ds(0, 4 * (Z - 1))], fn_r.at[0]
    ).wait()
    for r in range(Z):
        parts = [sto[0] if r == 0 else sti[r]]
        for kind in (1, 2, 3):
            parts.append(sto[r] if far_blocks[kind - 1] == r else sti[kind * Z + r])
        top, total, moment = merge(parts)
        inverse = 1.0 / total
        for n, value in enumerate((top, inverse, moment * inverse)):
            fin[r, n : n + 1, :] = jnp.concatenate([value[0:1, :], value[1:2, :]], axis=1)

    def z_sum(d, i, what, h):
        return copy(
            zs.at[d, i, what, h], zr.at[d, i, what, h], za_s.at[d, i, what, h], za_r.at[d, i, what, h],
            z_right if d == 0 else z_left,
        )

    def z_part(r, what, h):
        rows = slice(h * 64, (h + 1) * 64)
        later = slice(HD + h * 64, HD + (h + 1) * 64)
        scale = jnp.exp2((run[r, 0:1, :] - fin[r, 0:1, :]) * ALPHA) * fin[r, 1:2, :]
        if what == 0:
            return accv[r, rows, :] * scale
        return (accw[r, rows, :] - fin[r, 2:3, :] * accv[r, later, :]) * (scale * INV_ROOT)

    def z_add(i, order=(1, 0)):
        for short in order:
            for h in range(2):
                for d in range(2):
                    what = 1 - d if short else d
                    r = 4 + i if d == 0 else 4 - i
                    part = z_part(r, what, h)
                    if i > short:
                        z_sum(d, i - 1, what, h).wait_recv()
                        part = part + zr[d, i - 1, what, h].astype(F32)
                    zs[d, i, what, h] = part.astype(BF16)
                    send(z_sum(d, i, what, h))

    def sib_send(s):
        return copy(sbs.at[s], sbr.at[s], sb_s.at[s], sb_r.at[s], sib)

    mine = pl.ds(pl.multiple_of(core * T, T), T)
    other = pl.ds(pl.multiple_of((1 - core) * T, T), T)

    def factors(r, which):
        scale = jnp.exp2((pst[r, which, 0:1, :] - fin[r, 0:1, :]) * ALPHA) * fin[r, 1:2, :]
        root = scale * INV_ROOT
        shift = root * (pst[r, which, 1:2, :] - fin[r, 2:3, :])
        q = qt[r].astype(F32)
        return (
            (gt[r].astype(F32) * scale).astype(BF16),
            (q * shift).astype(BF16),
            (q * root).astype(BF16),
        )

    def sib_half(s):
        sbs[s] = kacc[s, :, other].astype(BF16)
        send(sib_send(s))

    def far_key(s):
        kacc[s] = jnp.zeros((2 * HD, C), F32)

        @pl.when(x >= s)
        def _():
            rows = slice(s * C, (s + 1) * C)
            kacc[s] = dot_nt(left_e[...], eb[rows, :])
            kacc[s, HD:, :] += dot_nt(left_t[...], tb[rows, :])

        sib_half(s)

    def near_key(s, r_low, r_high):
        kacc[s] = jnp.zeros((2 * HD, C), F32)

        def body(i, _):
            r = i % Z
            lanes = block_lanes(r)
            g_scaled, q_shift, q_root = factors(r, 0)
            sum_e = dot_nt(jnp.concatenate([g_scaled, q_shift], axis=0), eb[0:C, lanes])
            sum_t = dot_nt(q_root, tb[0:C, lanes])
            kacc[s, 0:HD, :] += sum_e[0:HD, :]
            kacc[s, HD:, :] += sum_e[HD:, :] + sum_t
            return 0

        lax.fori_loop(r_low, r_high, body, 0)
        sib_half(s)

    def own_part(s, what):
        rows = slice(what * HD, (what + 1) * HD)
        return kacc[s, rows, mine] + sbr[s, rows, :].astype(F32)

    x_target = [x_right, x_left, x_left, x_left, x_right, x_right]

    def x_sum(i):
        return copy(xs.at[i], xr.at[i], xr_s.at[i], xr_r.at[i], x_target[i])

    def x_send(i, part):
        xs[i] = part.astype(BF16)
        send(x_sum(i))

    z_add(0, (0,))
    z_add(1, (1,))

    @pl.when(x >= 1)
    def _():
        def scale_left(r, _):
            lanes = block_lanes(r)
            left_e[0:HD, lanes], left_e[HD:, lanes], left_t[:, lanes] = factors(r, 1)
            return 0

        lax.fori_loop(0, Z, scale_left, 0)

    far_key(2)
    far_key(1)
    sib_send(2).wait_recv()
    x_send(0, own_part(2, 0))
    x_send(1, own_part(2, 1))
    z_add(1, (0,))
    near_key(3, 4, jnp.where(x == X - 1, z + 1, 4))
    sib_send(1).wait_recv()
    x_send(2, own_part(1, 0))
    sib_send(3).wait_recv()
    x_send(5, own_part(3, 1))
    z_add(2)
    near_key(0, z + 1, Z + 1)
    x_sum(1).wait_recv()
    x_send(3, own_part(1, 1) + xr[1].astype(F32))
    x_sum(0).wait_recv()
    x_send(4, own_part(3, 0) + xr[0].astype(F32))
    z_add(3)

    def leave(i):
        return pltpu.make_async_copy(out_v.at[i], out_ref.at[i], out_s.at[i])

    sib_send(0).wait_recv()
    for what, near in ((0, (2, 4)), (1, (3, 5))):
        part = own_part(0, what)
        for i in near:
            x_sum(i).wait_recv()
            part = part + xr[i].astype(F32)
        out_v[3 - what] = part.T.astype(BF16)
        leave(3 - what).start()

    for hops in (*q_right, *q_left, *g_right, *g_left):
        for op in hops:
            op.wait_send()
    for op in (*k_sib, *v_sib, k_right, v_right, k_left, v_left, k_far, v_far):
        op.wait_send()
    for r in (1, 7, 2, 6):
        stat_send(r).wait_send()
    pltpu.make_async_copy(
        sti.at[pl.ds(0, 4 * (Z - 1))], sti.at[pl.ds(0, 4 * (Z - 1))], fn_s.at[0]
    ).wait()
    for op in started:
        op.wait_send()

    for what in range(2):
        halves = []
        for h in range(2):
            part = z_part(0, what, h)
            for d in range(2):
                z_sum(d, 3, what, h).wait_recv()
                part = part + zr[d, 3, what, h].astype(F32)
            halves.append(part)
        out_v[what] = jnp.concatenate(halves, axis=0).T.astype(BF16)
        leave(what).start()
    for i in range(4):
        leave(i).wait()


def hand_on(all_ref, *outs):
    for i, out in enumerate(outs):
        out[...] = all_ref[i]


def per_device(queries, keys, values, out_grad, segments):
    place = pl.BlockSpec(memory_space=pl.ANY)
    vmem = pl.BlockSpec(memory_space=pltpu.VMEM)
    dma = pltpu.SemaphoreType.DMA
    sums = pl.pallas_call(
        kernel,
        out_shape=jax.ShapeDtypeStruct((4, T, HD), BF16),
        in_specs=[place] * 5,
        out_specs=place,
        scratch_shapes=[
            pltpu.VMEM((T // HD, HD), jnp.int32),
            pltpu.VMEM((SEG_ROWS, HD), F32),
            pltpu.VMEM((4, T, HD), BF16),
            pltpu.VMEM((Z, T + SEG_ROWS, HD), BF16),
            pltpu.VMEM((Z, T, HD), BF16),
            pltpu.VMEM((Z, HD, T), BF16),
            pltpu.VMEM((Z, HD, T), BF16),
            pltpu.VMEM((X, 2, T + SEG_ROWS, HD), BF16),
            pltpu.VMEM((X, 2, T, HD), BF16),
            pltpu.VMEM((2 * HD, X * C), BF16),
            pltpu.VMEM((3 * C, Z * T), BF16),
            pltpu.VMEM((3 * C, Z * T), BF16),
            pltpu.VMEM((4, T, T), F32),
            pltpu.VMEM((4, T, T), F32),
            pltpu.VMEM((Z, 2, 8, T), F32),
            pltpu.VMEM((Z, 8, T), F32),
            pltpu.VMEM((Z, 2 * HD, T), F32),
            pltpu.VMEM((Z, HD, T), F32),
            pltpu.VMEM((2 * HD, Z * T), BF16),
            pltpu.VMEM((HD, Z * T), BF16),
            pltpu.VMEM((X, 2 * HD, C), F32),
            pltpu.VMEM((X, 16, T), F32),
            pltpu.VMEM((Z, 8, HD), F32),
            pltpu.VMEM((5 * Z, 8, HD), F32),
            pltpu.VMEM((Z, 8, T), F32),
            pltpu.VMEM((2, 4, 2, 2, HD // 2, T), BF16),
            pltpu.VMEM((2, 4, 2, 2, HD // 2, T), BF16),
            pltpu.VMEM((X, 2 * HD, T), BF16),
            pltpu.VMEM((X, 2 * HD, T), BF16),
            pltpu.VMEM((6, HD, T), BF16),
            pltpu.VMEM((6, HD, T), BF16),
            dma((Z, 2)), dma((Z, 2)), dma((Z, 2)), dma((Z, 2)),
            dma((14,)), dma((14,)),
            dma((Z,)), dma((Z,)), dma((1,)), dma((1,)),
            dma((2, 4, 2, 2)), dma((2, 4, 2, 2)),
            dma((X,)), dma((X,)), dma((6,)), dma((6,)), dma((5,)), dma((4,)),
        ],
        compiler_params=pltpu.CompilerParams(
            collective_id=0, has_side_effects=True, vmem_limit_bytes=58 * 1024 * 1024
        ),
        cost_estimate=pl.CostEstimate(
            flops=4 * 10**9, bytes_accessed=600_000, transcendentals=2 * 10**6
        ),
    )(queries, keys, values, out_grad, segments.reshape(T // HD, HD))
    return pl.pallas_call(
        hand_on,
        out_shape=(jax.ShapeDtypeStruct((T, HD), BF16),) * 4,
        in_specs=[vmem],
        out_specs=(vmem,) * 4,
    )(sums)


def solution(mesh):
    rows = P(("dp", "ctx"), None)
    return jax.shard_map(
        per_device,
        mesh=mesh,
        in_specs=(rows, rows, rows, rows, P(("dp", "ctx"))),
        out_specs=(rows, rows, rows, rows),
        check_vma=False,
    )
```

```python
import functools
import math

import jax
import jax.numpy as jnp
from jax import lax
from jax.experimental import pallas as pl
from jax.experimental.pallas import tpu as pltpu
from jax.sharding import PartitionSpec as P

MESH = pl.DeviceIdType.MESH
HD = 128
X, Z = 4, 8
T = 256
C = 2 * T
SEG_ROWS = 16
NEG = -1e30
INV_ROOT = 1.0 / math.sqrt(HD)
ALPHA = INV_ROOT * math.log2(math.e)
F32 = jnp.float32
BF16 = jnp.bfloat16
NT = (((1,), (1,)), ((), ()))


def dot_nt(a, b):
    return lax.dot_general(a, b, NT, preferred_element_type=F32)


def dot(a, b):
    return jnp.dot(a, b, preferred_element_type=F32)


def pick(index, values):
    result = values[-1]
    for i in range(len(values) - 2, -1, -1):
        result = jnp.where(index == i, values[i], result)
    return result


def kernel(
    q_ref, k_ref, v_ref, g_ref, seg_ref, out_ref,
    segi, segf, out_v, qs, gs, qt, gt, ks, vs, vkt, eb, tb, sbuf, dbuf, pst, run, accv, accw,
    left_e, left_t, kacc, cnt, sto, sti, fin, zs, zr, sbs, sbr, xs, xr,
    zq_s, zq_r, zg_s, zg_r, kv_s, kv_r, st_s, st_r, fn_s, fn_r,
    za_s, za_r, sb_s, sb_r, xr_s, xr_r, in_s, out_s,
):
    ctx = lax.axis_index("ctx")
    x = ctx // (2 * Z)
    z = (ctx // 2) % Z
    core = ctx % 2

    def dev(xx, zz, cc):
        return {"ctx": ((xx + X) % X) * (2 * Z) + ((zz + Z) % Z) * 2 + cc}

    sib = dev(x, z, 1 - core)
    z_right, z_left = dev(x, z + 1, core), dev(x, z - 1, core)
    x_right, x_left = dev(x + 1, z, core), dev(x - 1, z, core)

    barrier = pltpu.get_barrier_semaphore()
    for peer in (z_right, z_left, x_right, x_left, sib):
        pl.semaphore_signal(barrier, inc=1, device_id=peer, device_id_type=MESH)

    loads = [
        pltpu.make_async_copy(src, dst, in_s.at[i])
        for i, (src, dst) in enumerate((
            (seg_ref, segi),
            (q_ref, qs.at[0, 0:T, :]),
            (k_ref, ks.at[0, core, 0:T, :]),
            (v_ref, vs.at[0, core]),
            (g_ref, gs.at[0]),
        ))
    ]
    for op in loads:
        op.start()
    segf[...] = jnp.zeros_like(segf)
    run[0:1, :] = jnp.full((1, Z * T), NEG, F32)
    run[1:8, :] = jnp.zeros((7, Z * T), F32)
    loads[0].wait()
    segf[0 : T // HD, :] = segi[...].astype(F32)
    seg_rows = segf[...].astype(BF16)
    qs[0, T : T + SEG_ROWS, :] = seg_rows
    ks[0, core, T : T + SEG_ROWS, :] = seg_rows
    for op in loads[1:]:
        op.wait()

    pl.semaphore_wait(barrier, 5)

    def copy(src, dst, send, recv, target):
        return pltpu.make_async_remote_copy(
            src_ref=src, dst_ref=dst, send_sem=send, recv_sem=recv,
            device_id=target, device_id_type=MESH,
        )

    started = []

    def send(op):
        op.start()
        started.append(op)

    half = (slice(0, T + SEG_ROWS),)

    def q_hop(src, dst, target, h):
        return copy(
            qs.at[src, half[h], :], qs.at[dst, half[h], :], zq_s.at[dst, h], zq_r.at[dst, h], target
        )

    def g_hop(src, dst, target, h):
        rows = slice(h * 256, (h + 1) * 256)
        return copy(gs.at[src, rows, :], gs.at[dst, rows, :], zg_s.at[dst, h], zg_r.at[dst, h], target)

    def k_hop(i, src, dst, target):
        return copy(ks.at[src, core], ks.at[dst, core], kv_s.at[i], kv_r.at[i], target)

    def v_hop(i, src, dst, target):
        return copy(vs.at[src, core], vs.at[dst, core], kv_s.at[i], kv_r.at[i], target)

    q_right = [[q_hop(j, j + 1, z_right, h) for h in range(1)] for j in range(4)]
    q_left = [[q_hop((8 - j) % 8, 7 - j, z_left, h) for h in range(1)] for j in range(3)]
    g_right = [[g_hop(j, j + 1, z_right, h) for h in range(1)] for j in range(3)]
    g_left = [[g_hop((8 - j) % 8, 7 - j, z_left, h) for h in range(1)] for j in range(4)]
    k_sib = [k_hop(s, s, s, sib) for s in range(4)]
    v_sib = [v_hop(4 + s, s, s, sib) for s in range(4)]
    k_right, v_right = k_hop(8, 0, 1, x_right), v_hop(9, 0, 1, x_right)
    k_left, v_left = k_hop(10, 0, 3, x_left), v_hop(11, 0, 3, x_left)
    k_far, v_far = k_hop(12, 1, 2, x_right), v_hop(13, 3, 2, x_left)

    for op in (q_right[0][0], g_left[0][0], k_right, v_left, k_sib[0], v_sib[0]):
        op.start()
    for h in range(1, 1):
        q_right[0][h].start()
        g_left[0][h].start()
    v_right.start()
    k_left.start()
    for h in range(1):
        g_right[0][h].start()
        q_left[0][h].start()

    def z_step(j, which):
        for h in range(1):
            for hops in ((q_right, g_left), (g_right, q_left))[which]:
                if j <= len(hops):
                    hops[j - 1][h].wait_recv()
                if j < len(hops):
                    hops[j][h].start()

    doc16 = lax.broadcasted_iota(jnp.int32, (16, HD), 0).astype(F32)

    def prepare_keys(s):
        below = jnp.zeros((16, HD), F32)
        for c in range(2):
            lanes = slice(s * C + c * T, s * C + (c + 1) * T)
            vkt[0:HD, lanes] = vs[s, c].T
            vkt[HD:, lanes] = ks[s, c, 0:T, :].T
            seg = ks[s, c, T : T + SEG_ROWS, :].astype(F32)
            for h in range(T // HD):
                below += jnp.where(seg[h : h + 1, :] < doc16, 1.0, 0.0)
        cnt[s] = jnp.broadcast_to(jnp.sum(below, axis=1, keepdims=True), (16, T))

    def prepare_queries(r):
        qt[:, r * T : (r + 1) * T] = qs[r, 0:T, :].T
        gt[:, r * T : (r + 1) * T] = gs[r].T

    key_row = lax.broadcasted_iota(jnp.int32, (T, T), 0).astype(F32)
    query_lane = lax.broadcasted_iota(jnp.int32, (1, T), 1).astype(F32)
    doc_q = lax.broadcasted_iota(jnp.int32, (16, T), 0).astype(F32)

    def near_slot(r):
        own = (r == 0) | (r > z)
        used = own | ((x == X - 1) & (r >= 4))
        return used, jnp.where(own, 0, 3)

    def block_lanes(r):
        return pl.ds(pl.multiple_of(r * T, T), T)

    def piece(blocks, which, chunks, diagonal=False):
        tops, lows = [], []
        for n, r in enumerate(blocks):
            seg = qs[r, T : T + SEG_ROWS, :].astype(F32)
            same = jnp.concatenate([seg[0:1, :], seg[1:2, :]], axis=1) == doc_q
            low = [jnp.sum(jnp.where(same, cnt[s], 0.0), axis=0, keepdims=True) for _, s in chunks]
            lows.append([jnp.where(x >= 2, v, 1e9) if u == 2 else v for v, (u, _) in zip(low, chunks)])
            tops.append(run[0:1, block_lanes(r)])
        parts = [(i, s, c, u * C + c * T) for i, (u, s) in enumerate(chunks) for c in range(2)]
        for b, (i, s, c, row) in enumerate(parts):
            for n, r in enumerate(blocks):
                sc = dot_nt(ks[s, c, 0:T, :], qs[r, 0:T, :])
                allowed = key_row >= lows[n][i] - c * T
                if diagonal:
                    allowed = allowed & (key_row <= query_lane + ((core - c) * T).astype(F32))
                sc = jnp.where(allowed, sc, NEG)
                sbuf[n, b] = sc
                tops[n] = jnp.maximum(tops[n], jnp.max(sc, axis=0, keepdims=True))
        totals = [jnp.zeros((1, T), F32) for _ in blocks]
        moments = [jnp.zeros((1, T), F32) for _ in blocks]
        for b, (i, s, c, row) in enumerate(parts):
            for n, r in enumerate(blocks):
                e = jnp.exp2((sbuf[n, b] - tops[n]) * ALPHA)
                weighted = e * dot_nt(vs[s, c], gs[r])
                eb[row : row + T, block_lanes(r)] = e.astype(BF16)
                sbuf[n, b] = e
                dbuf[n, b] = weighted
                totals[n] += jnp.sum(e, axis=0, keepdims=True)
                moments[n] += jnp.sum(weighted, axis=0, keepdims=True)
        means = [moment / jnp.maximum(total, 1e-30) for moment, total in zip(moments, totals)]
        for b, (i, s, c, row) in enumerate(parts):
            for n, r in enumerate(blocks):
                tb[row : row + T, block_lanes(r)] = (dbuf[n, b] - sbuf[n, b] * means[n]).astype(BF16)
        for n, r in enumerate(blocks):
            lanes = block_lanes(r)
            pst[which, 0:1, lanes] = tops[n]
            pst[which, 1:2, lanes] = means[n]
            keep = jnp.exp2((run[0:1, lanes] - tops[n]) * ALPHA)
            run[0:1, lanes] = tops[n]
            run[1:2, lanes] = run[1:2, lanes] * keep + totals[n]
            run[2:3, lanes] = run[2:3, lanes] * keep + moments[n]

    def near_products(r, s):
        lanes = block_lanes(r)
        keys = pl.ds(pl.multiple_of(s * C, C), C)
        part_v = dot(vkt[:, keys], eb[0:C, lanes])
        part_t = dot(vkt[HD:, keys], tb[0:C, lanes])
        accv[:, lanes] = part_v
        accw[:, lanes] = part_t + pst[0, 1:2, lanes] * part_v[HD:, :]

    def far_products(lanes):
        part_v = dot(vkt[:, C : 3 * C], eb[C : 3 * C, lanes])
        part_t = dot(vkt[HD:, C : 3 * C], tb[C : 3 * C, lanes])
        keep = jnp.exp2((pst[0, 0:1, lanes] - run[0:1, lanes]) * ALPHA)
        accv[:, lanes] = accv[:, lanes] * keep + part_v
        accw[:, lanes] = accw[:, lanes] * keep + part_t + pst[1, 1:2, lanes] * part_v[HD:, :]

    def near_piece(r, multiply):
        used, s = near_slot(r)

        @pl.when(used)
        def _():
            piece([r], 0, [(0, s)])
            if multiply:
                near_products(r, s)

        @pl.when(jnp.logical_not(used))
        def _():
            lanes = block_lanes(r)
            eb[0:C, lanes] = jnp.zeros((C, T), BF16)
            tb[0:C, lanes] = jnp.zeros((C, T), BF16)
            pst[0, 0:1, lanes] = jnp.full((1, T), NEG, F32)
            pst[0, 1:2, lanes] = jnp.zeros((1, T), F32)
            accv[:, lanes] = jnp.zeros((2 * HD, T), F32)
            accw[:, lanes] = jnp.zeros((HD, T), F32)

    lane_block = lax.broadcasted_iota(jnp.int32, (1, Z * T), 1) // T
    own_lanes = (lane_block == 0) | (lane_block > z)
    upper = slice(4 * T, Z * T)

    def pack(i, values):
        for n in range(3):
            for h in range(2):
                sto[i, 2 * n + h : 2 * n + h + 1, :] = values[n][:, h * HD : (h + 1) * HD]

    def merge(parts):
        top = functools.reduce(jnp.maximum, [p[0:2, :] for p in parts])
        scales = [jnp.exp2((p[0:2, :] - top) * ALPHA) for p in parts]
        total = sum(p[2:4, :] * scale for p, scale in zip(parts, scales))
        moment = sum(p[4:6, :] * scale for p, scale in zip(parts, scales))
        return top, total, moment

    def stat_send(r):
        return copy(sto.at[r], sti.at[32 + r], st_s.at[r], st_r.at[r], dev(x, z - r, core))

    far_blocks = (3, 5, 4)

    def total_send(kind, d):
        r = 0 if kind == 0 else far_blocks[kind - 1]
        slot = kind * Z + (d + r) % Z
        return copy(sto.at[r], sti.at[slot], fn_s.at[0], fn_r.at[0], dev(x, z + d, core))

    prepare_queries(0)
    k_sib[0].wait_recv()
    v_sib[0].wait_recv()
    prepare_keys(0)
    piece([0], 0, [(0, 0)], diagonal=True)
    near_products(0, 0)

    z_step(1, 0)
    k_right.wait_recv()
    k_far.start()
    k_sib[1].start()
    v_left.wait_recv()
    v_far.start()
    v_sib[3].start()
    z_step(1, 1)
    v_right.wait_recv()
    v_sib[1].start()
    k_left.wait_recv()
    k_sib[3].start()
    prepare_queries(1)
    prepare_queries(7)
    z_step(2, 0)
    for s in (1, 3):
        k_sib[s].wait_recv()
        v_sib[s].wait_recv()
        prepare_keys(s)

    def early(i, _):
        @pl.when(i == 1)
        def _():
            k_far.wait_recv()
            k_sib[2].start()
            v_far.wait_recv()
            v_sib[2].start()

        @pl.when(i == 2)
        def _():
            z_step(2, 1)
            prepare_queries(2)
            prepare_queries(6)

        near_piece(pick(i, [1, 7, 2, 6]), True)
        return 0

    lax.fori_loop(0, 4, early, 0)
    z_step(3, 0)
    k_sib[2].wait_recv()
    v_sib[2].wait_recv()
    prepare_keys(2)

    def block(i, _):
        @pl.when(i == 2)
        def _():
            z_step(3, 1)

        r = pick(i, [0, 1, 7, 2, 6])

        @pl.when(x >= 1)
        def _():
            piece([r], 1, [(1, 1), (2, 2)])

        @pl.when(i > 0)
        def _():
            pack(r, [run[n : n + 1, block_lanes(r)] for n in range(3)])
            stat_send(r).start()

        return 0

    lax.fori_loop(0, 5, block, 0)

    def late_block(i, _):
        @pl.when(i == 2)
        def _():
            for r in (1, 7, 2, 6):
                stat_send(r).wait_recv()
            own = [run[n : n + 1, 0:T] for n in range(3)]
            pack(0, own)
            merged = merge([sto[0]] + [sti[32 + r] for r in (1, 7, 2, 6)])
            for n in range(3):
                sto[0, 2 * n : 2 * n + 2, :] = merged[n]
            for d in (3, 5, 2, 6, 1, 7):
                total_send(0, d).start()
            z_step(4, 0)
            for kind in range(3):
                total_send(kind, 4).start()

        r = pick(i, [3, 5, 4])
        near_piece(r, False)
        used, s = near_slot(r)

        @pl.when((i < 2) & used)
        def _():
            near_products(r, s)

        @pl.when(x >= 1)
        def _():
            piece([r], 1, [(1, 1), (2, 2)])

        pack(r, [run[n : n + 1, block_lanes(r)] for n in range(3)])

        for kind in (1, 2):

            @pl.when(i == kind - 1)
            def _():
                for d in (3, 5, 2, 6, 1, 7):
                    total_send(kind, d).start()

        return 0

    lax.fori_loop(0, 3, late_block, 0)
    for d in (4, 3, 5, 2, 6, 1, 7):
        total_send(3, d).start()


    used, s_zero = near_slot(4)

    @pl.when(used)
    def _():
        near_products(4, s_zero)

    @pl.when(x >= 1)
    def _():
        def body(i, _):
            far_products(pl.ds(pl.multiple_of(i * 2 * T, 2 * T), 2 * T))
            return 0

        lax.fori_loop(0, 4, body, 0)

    for r in (3, 5, 4):
        prepare_queries(r)

    pltpu.make_async_copy(
        sti.at[pl.ds(0, 4 * (Z - 1))], sti.at[pl.ds(0, 4 * (Z - 1))], fn_r.at[0]
    ).wait()
    for r in range(Z):
        parts = [sto[0] if r == 0 else sti[r]]
        for kind in (1, 2, 3):
            parts.append(sto[r] if far_blocks[kind - 1] == r else sti[kind * Z + r])
        top, total, moment = merge(parts)
        inverse = 1.0 / total
        for n, value in enumerate((top, inverse, moment * inverse)):
            fin[n : n + 1, r * T : (r + 1) * T] = jnp.concatenate([value[0:1, :], value[1:2, :]], axis=1)

    def z_sum(d, i, what, h):
        return copy(
            zs.at[d, i, what, h], zr.at[d, i, what, h], za_s.at[d, i, what, h], za_r.at[d, i, what, h],
            z_right if d == 0 else z_left,
        )

    def z_part(r, what, h):
        rows = slice(h * 128, (h + 1) * 128)
        later = slice(HD + h * 128, HD + (h + 1) * 128)
        lanes = slice(r * T, (r + 1) * T)
        scale = jnp.exp2((run[0:1, lanes] - fin[0:1, lanes]) * ALPHA) * fin[1:2, lanes]
        if what == 0:
            return accv[rows, lanes] * scale
        return (accw[rows, lanes] - fin[2:3, lanes] * accv[later, lanes]) * (scale * INV_ROOT)

    def z_add(i, order=(1, 0)):
        for short in order:
            for h in range(1):
                for d in range(2):
                    what = 1 - d if short else d
                    r = 4 + i if d == 0 else 4 - i
                    part = z_part(r, what, h)
                    if i > short:
                        z_sum(d, i - 1, what, h).wait_recv()
                        part = part + zr[d, i - 1, what, h].astype(F32)
                    zs[d, i, what, h] = part.astype(BF16)
                    send(z_sum(d, i, what, h))

    def sib_send(s):
        return copy(sbs.at[s], sbr.at[s], sb_s.at[s], sb_r.at[s], sib)

    mine = pl.ds(pl.multiple_of(core * T, T), T)
    other = pl.ds(pl.multiple_of((1 - core) * T, T), T)

    def scale_left(which, lanes, valid):
        scale = jnp.exp2((pst[which, 0:1, lanes] - fin[0:1, lanes]) * ALPHA) * fin[1:2, lanes]
        if valid is not None:
            scale = jnp.where(valid, scale, 0.0)
        root = scale * INV_ROOT
        shift = root * (pst[which, 1:2, lanes] - fin[2:3, lanes])
        q = qt[:, lanes].astype(F32)
        left_e[0:HD, lanes] = (gt[:, lanes].astype(F32) * scale).astype(BF16)
        left_e[HD:, lanes] = (q * shift).astype(BF16)
        left_t[:, lanes] = (q * root).astype(BF16)

    def sib_half(s):
        sbs[s] = kacc[s, :, other].astype(BF16)
        send(sib_send(s))

    def key_products(s, rows, lanes):
        kacc[s] = dot_nt(left_e[:, lanes], eb[rows, lanes])
        kacc[s, HD:, :] += dot_nt(left_t[:, lanes], tb[rows, lanes])

    def far_key(s):
        @pl.when(x >= s)
        def _():
            rows = slice(s * C, (s + 1) * C)
            key_products(s, rows, slice(0, Z * T))

        @pl.when(x < s)
        def _():
            kacc[s] = jnp.zeros((2 * HD, C), F32)

        sib_half(s)

    def own_part(s, what):
        rows = slice(what * HD, (what + 1) * HD)
        return kacc[s, rows, mine] + sbr[s, rows, :].astype(F32)

    x_target = [x_right, x_left, x_left, x_left, x_right, x_right]

    def x_sum(i):
        return copy(xs.at[i], xr.at[i], xr_s.at[i], xr_r.at[i], x_target[i])

    def x_send(i, part):
        xs[i] = part.astype(BF16)
        send(x_sum(i))

    z_add(0, (0,))
    z_add(1, (1,))

    @pl.when(x >= 1)
    def _():
        scale_left(1, slice(0, Z * T), None)

    far_key(2)
    far_key(1)
    sib_send(2).wait_recv()
    x_send(0, own_part(2, 0))
    x_send(1, own_part(2, 1))
    z_add(1, (0,))

    @pl.when(x == X - 1)
    def _():
        scale_left(0, upper, jnp.logical_not(own_lanes)[:, upper])
        key_products(3, slice(0, C), upper)

    @pl.when(x < X - 1)
    def _():
        kacc[3] = jnp.zeros((2 * HD, C), F32)

    sib_half(3)
    sib_send(1).wait_recv()
    x_send(2, own_part(1, 0))
    sib_send(3).wait_recv()
    x_send(5, own_part(3, 1))
    z_add(2)
    scale_left(0, slice(0, Z * T), own_lanes)
    key_products(0, slice(0, C), slice(0, Z * T))
    sib_half(0)
    x_sum(1).wait_recv()
    x_send(3, own_part(1, 1) + xr[1].astype(F32))
    x_sum(0).wait_recv()
    x_send(4, own_part(3, 0) + xr[0].astype(F32))
    z_add(3)

    def leave(i):
        return pltpu.make_async_copy(out_v.at[i], out_ref.at[i], out_s.at[i])

    sib_send(0).wait_recv()
    for what, near in ((0, (2, 4)), (1, (3, 5))):
        part = own_part(0, what)
        for i in near:
            x_sum(i).wait_recv()
            part = part + xr[i].astype(F32)
        out_v[3 - what] = part.T.astype(BF16)
        leave(3 - what).start()

    for hops in (*q_right, *q_left, *g_right, *g_left):
        for op in hops:
            op.wait_send()
    for op in (*k_sib, *v_sib, k_right, v_right, k_left, v_left, k_far, v_far):
        op.wait_send()
    for r in (1, 7, 2, 6):
        stat_send(r).wait_send()
    pltpu.make_async_copy(
        sti.at[pl.ds(0, 4 * (Z - 1))], sti.at[pl.ds(0, 4 * (Z - 1))], fn_s.at[0]
    ).wait()
    for op in started:
        op.wait_send()

    for what in range(2):
        halves = []
        for h in range(1):
            part = z_part(0, what, h)
            for d in range(2):
                z_sum(d, 3, what, h).wait_recv()
                part = part + zr[d, 3, what, h].astype(F32)
            halves.append(part)
        out_v[what] = jnp.concatenate(halves, axis=0).T.astype(BF16)
        leave(what).start()
    for i in range(4):
        leave(i).wait()


def hand_on(all_ref, *outs):
    for i, out in enumerate(outs):
        out[...] = all_ref[i]


def per_device(queries, keys, values, out_grad, segments):
    place = pl.BlockSpec(memory_space=pl.ANY)
    vmem = pl.BlockSpec(memory_space=pltpu.VMEM)
    dma = pltpu.SemaphoreType.DMA
    sums = pl.pallas_call(
        kernel,
        out_shape=jax.ShapeDtypeStruct((4, T, HD), BF16),
        in_specs=[place] * 5,
        out_specs=place,
        scratch_shapes=[
            pltpu.VMEM((T // HD, HD), jnp.int32),
            pltpu.VMEM((SEG_ROWS, HD), F32),
            pltpu.VMEM((4, T, HD), BF16),
            pltpu.VMEM((Z, T + SEG_ROWS, HD), BF16),
            pltpu.VMEM((Z, T, HD), BF16),
            pltpu.VMEM((HD, Z * T), BF16),
            pltpu.VMEM((HD, Z * T), BF16),
            pltpu.VMEM((X, 2, T + SEG_ROWS, HD), BF16),
            pltpu.VMEM((X, 2, T, HD), BF16),
            pltpu.VMEM((2 * HD, X * C), BF16),
            pltpu.VMEM((3 * C, Z * T), BF16),
            pltpu.VMEM((3 * C, Z * T), BF16),
            pltpu.VMEM((2, 4, T, T), F32),
            pltpu.VMEM((2, 4, T, T), F32),
            pltpu.VMEM((2, 8, Z * T), F32),
            pltpu.VMEM((8, Z * T), F32),
            pltpu.VMEM((2 * HD, Z * T), F32),
            pltpu.VMEM((HD, Z * T), F32),
            pltpu.VMEM((2 * HD, Z * T), BF16),
            pltpu.VMEM((HD, Z * T), BF16),
            pltpu.VMEM((X, 2 * HD, C), F32),
            pltpu.VMEM((X, 16, T), F32),
            pltpu.VMEM((Z, 8, HD), F32),
            pltpu.VMEM((5 * Z, 8, HD), F32),
            pltpu.VMEM((8, Z * T), F32),
            pltpu.VMEM((2, 4, 2, 1, HD // 1, T), BF16),
            pltpu.VMEM((2, 4, 2, 1, HD // 1, T), BF16),
            pltpu.VMEM((X, 2 * HD, T), BF16),
            pltpu.VMEM((X, 2 * HD, T), BF16),
            pltpu.VMEM((6, HD, T), BF16),
            pltpu.VMEM((6, HD, T), BF16),
            dma((Z, 1)), dma((Z, 1)), dma((Z, 1)), dma((Z, 1)),
            dma((14,)), dma((14,)),
            dma((Z,)), dma((Z,)), dma((1,)), dma((1,)),
            dma((2, 4, 2, 1)), dma((2, 4, 2, 1)),
            dma((X,)), dma((X,)), dma((6,)), dma((6,)), dma((5,)), dma((4,)),
        ],
        compiler_params=pltpu.CompilerParams(
            collective_id=0, has_side_effects=True, vmem_limit_bytes=58 * 1024 * 1024
        ),
        cost_estimate=pl.CostEstimate(
            flops=4 * 10**9, bytes_accessed=600_000, transcendentals=2 * 10**6
        ),
    )(queries, keys, values, out_grad, segments.reshape(T // HD, HD))
    return tuple(sums[i] for i in range(4))


def solution(mesh):
    rows = P(("dp", "ctx"), None)
    return jax.shard_map(
        per_device,
        mesh=mesh,
        in_specs=(rows, rows, rows, rows, P(("dp", "ctx"))),
        out_specs=(rows, rows, rows, rows),
        check_vma=False,
    )
```

```python
import functools
import math

import jax
import jax.numpy as jnp
from jax import lax
from jax.experimental import pallas as pl
from jax.experimental.pallas import tpu as pltpu
from jax.sharding import PartitionSpec as P

MESH = pl.DeviceIdType.MESH
HD = 128
X, Z = 4, 8
T = 256
C = 2 * T
SEG_ROWS = 16
NEG = -1e30
INV_ROOT = 1.0 / math.sqrt(HD)
ALPHA = INV_ROOT * math.log2(math.e)
F32 = jnp.float32
BF16 = jnp.bfloat16
NT = (((1,), (1,)), ((), ()))


def dot_nt(a, b):
    return lax.dot_general(a, b, NT, preferred_element_type=F32)


def dot(a, b):
    return jnp.dot(a, b, preferred_element_type=F32)


def pick(index, values):
    result = values[-1]
    for i in range(len(values) - 2, -1, -1):
        result = jnp.where(index == i, values[i], result)
    return result


def kernel(
    q_ref, k_ref, v_ref, g_ref, seg_ref, out_ref,
    segi, segf, out_v, qs, gs, qt, gt, ks, vs, vkt, eb, tb, sbuf, dbuf, pst, run, accv, accw,
    left_e, left_t, kacc, cnt, sto, sti, fin, zs, zr, sbs, sbr, xs, xr,
    zq_s, zq_r, zg_s, zg_r, kv_s, kv_r, st_s, st_r, fn_s, fn_r,
    za_s, za_r, sb_s, sb_r, xr_s, xr_r, in_s, out_s,
):
    ctx = lax.axis_index("ctx")
    x = ctx // (2 * Z)
    z = (ctx // 2) % Z
    core = ctx % 2

    def dev(xx, zz, cc):
        return {"ctx": ((xx + X) % X) * (2 * Z) + ((zz + Z) % Z) * 2 + cc}

    sib = dev(x, z, 1 - core)
    z_right, z_left = dev(x, z + 1, core), dev(x, z - 1, core)
    x_right, x_left = dev(x + 1, z, core), dev(x - 1, z, core)

    barrier = pltpu.get_barrier_semaphore()
    for peer in (z_right, z_left, x_right, x_left, sib):
        pl.semaphore_signal(barrier, inc=1, device_id=peer, device_id_type=MESH)

    loads = [
        pltpu.make_async_copy(src, dst, in_s.at[i])
        for i, (src, dst) in enumerate((
            (seg_ref, segi),
            (q_ref, qs.at[0, 0:T, :]),
            (k_ref, ks.at[0, core, 0:T, :]),
            (v_ref, vs.at[0, core]),
            (g_ref, gs.at[0]),
        ))
    ]
    for op in loads:
        op.start()
    segf[...] = jnp.zeros_like(segf)
    run[0:1, :] = jnp.full((1, Z * T), NEG, F32)
    run[1:8, :] = jnp.zeros((7, Z * T), F32)
    loads[0].wait()
    segf[0 : T // HD, :] = segi[...].astype(F32)
    seg_rows = segf[...].astype(BF16)
    qs[0, T : T + SEG_ROWS, :] = seg_rows
    ks[0, core, T : T + SEG_ROWS, :] = seg_rows
    for op in loads[1:]:
        op.wait()

    pl.semaphore_wait(barrier, 5)

    def copy(src, dst, send, recv, target):
        return pltpu.make_async_remote_copy(
            src_ref=src, dst_ref=dst, send_sem=send, recv_sem=recv,
            device_id=target, device_id_type=MESH,
        )

    started = []

    def send(op):
        op.start()
        started.append(op)

    half = (slice(0, T + SEG_ROWS),)

    def q_hop(src, dst, target, h):
        return copy(
            qs.at[src, half[h], :], qs.at[dst, half[h], :], zq_s.at[dst, h], zq_r.at[dst, h], target
        )

    def g_hop(src, dst, target, h):
        rows = slice(h * 256, (h + 1) * 256)
        return copy(gs.at[src, rows, :], gs.at[dst, rows, :], zg_s.at[dst, h], zg_r.at[dst, h], target)

    def k_hop(i, src, dst, target):
        return copy(ks.at[src, core], ks.at[dst, core], kv_s.at[i], kv_r.at[i], target)

    def v_hop(i, src, dst, target):
        return copy(vs.at[src, core], vs.at[dst, core], kv_s.at[i], kv_r.at[i], target)

    q_right = [[q_hop(j, j + 1, z_right, h) for h in range(1)] for j in range(4)]
    q_left = [[q_hop((8 - j) % 8, 7 - j, z_left, h) for h in range(1)] for j in range(3)]
    g_right = [[g_hop(j, j + 1, z_right, h) for h in range(1)] for j in range(3)]
    g_left = [[g_hop((8 - j) % 8, 7 - j, z_left, h) for h in range(1)] for j in range(4)]
    k_sib = [k_hop(s, s, s, sib) for s in range(4)]
    v_sib = [v_hop(4 + s, s, s, sib) for s in range(4)]
    k_right, v_right = k_hop(8, 0, 1, x_right), v_hop(9, 0, 1, x_right)
    k_left, v_left = k_hop(10, 0, 3, x_left), v_hop(11, 0, 3, x_left)
    k_far, v_far = k_hop(12, 1, 2, x_right), v_hop(13, 3, 2, x_left)

    for op in (q_right[0][0], g_left[0][0], k_right, v_left, k_sib[0], v_sib[0]):
        op.start()
    for h in range(1, 1):
        q_right[0][h].start()
        g_left[0][h].start()
    v_right.start()
    k_left.start()
    for h in range(1):
        g_right[0][h].start()
        q_left[0][h].start()

    def z_step(j, which):
        for h in range(1):
            for hops in ((q_right, g_left), (g_right, q_left))[which]:
                if j <= len(hops):
                    hops[j - 1][h].wait_recv()
                if j < len(hops):
                    hops[j][h].start()

    doc16 = lax.broadcasted_iota(jnp.int32, (16, HD), 0).astype(F32)

    def prepare_keys(s):
        below = jnp.zeros((16, HD), F32)
        for c in range(2):
            lanes = slice(s * C + c * T, s * C + (c + 1) * T)
            vkt[0:HD, lanes] = vs[s, c].T
            vkt[HD:, lanes] = ks[s, c, 0:T, :].T
            seg = ks[s, c, T : T + SEG_ROWS, :].astype(F32)
            for h in range(T // HD):
                below += jnp.where(seg[h : h + 1, :] < doc16, 1.0, 0.0)
        cnt[s] = jnp.broadcast_to(jnp.sum(below, axis=1, keepdims=True), (16, T))

    def prepare_queries(r):
        qt[:, r * T : (r + 1) * T] = qs[r, 0:T, :].T
        gt[:, r * T : (r + 1) * T] = gs[r].T

    key_row = lax.broadcasted_iota(jnp.int32, (T, T), 0).astype(F32)
    query_lane = lax.broadcasted_iota(jnp.int32, (1, T), 1).astype(F32)
    doc_q = lax.broadcasted_iota(jnp.int32, (16, T), 0).astype(F32)

    def near_slot(r):
        own = (r == 0) | (r > z)
        used = own | ((x == X - 1) & (r >= 4))
        return used, jnp.where(own, 0, 3)

    def block_lanes(r):
        return pl.ds(pl.multiple_of(r * T, T), T)

    def piece(blocks, which, chunks, diagonal=False):
        tops, lows = [], []
        for n, r in enumerate(blocks):
            seg = qs[r, T : T + SEG_ROWS, :].astype(F32)
            same = jnp.concatenate([seg[0:1, :], seg[1:2, :]], axis=1) == doc_q
            low = [jnp.sum(jnp.where(same, cnt[s], 0.0), axis=0, keepdims=True) for _, s in chunks]
            lows.append([jnp.where(x >= 2, v, 1e9) if u == 2 else v for v, (u, _) in zip(low, chunks)])
            tops.append(run[0:1, block_lanes(r)])
        parts = [(i, s, c, u * C + c * T) for i, (u, s) in enumerate(chunks) for c in range(2)]
        for b, (i, s, c, row) in enumerate(parts):
            for n, r in enumerate(blocks):
                sc = dot_nt(ks[s, c, 0:T, :], qs[r, 0:T, :])
                allowed = key_row >= lows[n][i] - c * T
                if diagonal:
                    allowed = allowed & (key_row <= query_lane + ((core - c) * T).astype(F32))
                sc = jnp.where(allowed, sc, NEG)
                sbuf[n, b] = sc
                tops[n] = jnp.maximum(tops[n], jnp.max(sc, axis=0, keepdims=True))
        totals = [jnp.zeros((1, T), F32) for _ in blocks]
        moments = [jnp.zeros((1, T), F32) for _ in blocks]
        for b, (i, s, c, row) in enumerate(parts):
            for n, r in enumerate(blocks):
                e = jnp.exp2((sbuf[n, b] - tops[n]) * ALPHA)
                weighted = e * dot_nt(vs[s, c], gs[r])
                eb[row : row + T, block_lanes(r)] = e.astype(BF16)
                sbuf[n, b] = e
                dbuf[n, b] = weighted
                totals[n] += jnp.sum(e, axis=0, keepdims=True)
                moments[n] += jnp.sum(weighted, axis=0, keepdims=True)
        means = [moment / jnp.maximum(total, 1e-30) for moment, total in zip(moments, totals)]
        for b, (i, s, c, row) in enumerate(parts):
            for n, r in enumerate(blocks):
                tb[row : row + T, block_lanes(r)] = (dbuf[n, b] - sbuf[n, b] * means[n]).astype(BF16)
        for n, r in enumerate(blocks):
            lanes = block_lanes(r)
            pst[which, 0:1, lanes] = tops[n]
            pst[which, 1:2, lanes] = means[n]
            keep = jnp.exp2((run[0:1, lanes] - tops[n]) * ALPHA)
            run[0:1, lanes] = tops[n]
            run[1:2, lanes] = run[1:2, lanes] * keep + totals[n]
            run[2:3, lanes] = run[2:3, lanes] * keep + moments[n]

    def near_products(r, s):
        lanes = block_lanes(r)
        keys = pl.ds(pl.multiple_of(s * C, C), C)
        part_v = dot(vkt[:, keys], eb[0:C, lanes])
        part_t = dot(vkt[HD:, keys], tb[0:C, lanes])
        accv[:, lanes] = part_v
        accw[:, lanes] = part_t + pst[0, 1:2, lanes] * part_v[HD:, :]

    def far_products(lanes):
        part_v = dot(vkt[:, C : 3 * C], eb[C : 3 * C, lanes])
        part_t = dot(vkt[HD:, C : 3 * C], tb[C : 3 * C, lanes])
        keep = jnp.exp2((pst[0, 0:1, lanes] - run[0:1, lanes]) * ALPHA)
        accv[:, lanes] = accv[:, lanes] * keep + part_v
        accw[:, lanes] = accw[:, lanes] * keep + part_t + pst[1, 1:2, lanes] * part_v[HD:, :]

    def near_piece(r, multiply):
        used, s = near_slot(r)

        @pl.when(used)
        def _():
            piece([r], 0, [(0, s)])
            if multiply:
                near_products(r, s)

        @pl.when(jnp.logical_not(used))
        def _():
            lanes = block_lanes(r)
            eb[0:C, lanes] = jnp.zeros((C, T), BF16)
            tb[0:C, lanes] = jnp.zeros((C, T), BF16)
            pst[0, 0:1, lanes] = jnp.full((1, T), NEG, F32)
            pst[0, 1:2, lanes] = jnp.zeros((1, T), F32)
            accv[:, lanes] = jnp.zeros((2 * HD, T), F32)
            accw[:, lanes] = jnp.zeros((HD, T), F32)

    lane_block = lax.broadcasted_iota(jnp.int32, (1, Z * T), 1) // T
    own_lanes = (lane_block == 0) | (lane_block > z)
    upper = slice(4 * T, Z * T)

    def pack(i, values):
        for n in range(3):
            for h in range(2):
                sto[i, 2 * n + h : 2 * n + h + 1, :] = values[n][:, h * HD : (h + 1) * HD]

    def merge(parts):
        top = functools.reduce(jnp.maximum, [p[0:2, :] for p in parts])
        scales = [jnp.exp2((p[0:2, :] - top) * ALPHA) for p in parts]
        total = sum(p[2:4, :] * scale for p, scale in zip(parts, scales))
        moment = sum(p[4:6, :] * scale for p, scale in zip(parts, scales))
        return top, total, moment

    def stat_send(r):
        return copy(sto.at[r], sti.at[32 + r], st_s.at[r], st_r.at[r], dev(x, z - r, core))

    far_blocks = (3, 5, 4)

    def total_send(kind, d):
        r = 0 if kind == 0 else far_blocks[kind - 1]
        slot = kind * Z + (d + r) % Z
        return copy(sto.at[r], sti.at[slot], fn_s.at[0], fn_r.at[0], dev(x, z + d, core))

    prepare_queries(0)
    k_sib[0].wait_recv()
    v_sib[0].wait_recv()
    prepare_keys(0)
    piece([0], 0, [(0, 0)], diagonal=True)
    near_products(0, 0)

    z_step(1, 0)
    k_right.wait_recv()
    k_far.start()
    k_sib[1].start()
    v_left.wait_recv()
    v_far.start()
    v_sib[3].start()
    z_step(1, 1)
    v_right.wait_recv()
    v_sib[1].start()
    k_left.wait_recv()
    k_sib[3].start()
    prepare_queries(1)
    prepare_queries(7)
    z_step(2, 0)
    for s in (1, 3):
        k_sib[s].wait_recv()
        v_sib[s].wait_recv()
        prepare_keys(s)

    def early(i, _):
        @pl.when(i == 1)
        def _():
            k_far.wait_recv()
            k_sib[2].start()
            v_far.wait_recv()
            v_sib[2].start()

        @pl.when(i == 2)
        def _():
            z_step(2, 1)
            prepare_queries(2)
            prepare_queries(6)

        near_piece(pick(i, [1, 7, 2, 6]), True)
        return 0

    lax.fori_loop(0, 4, early, 0)
    z_step(3, 0)
    k_sib[2].wait_recv()
    v_sib[2].wait_recv()
    prepare_keys(2)

    def block(i, _):
        @pl.when(i == 2)
        def _():
            z_step(3, 1)

        r = pick(i, [0, 1, 7, 2, 6])

        @pl.when(x >= 1)
        def _():
            piece([r], 1, [(1, 1), (2, 2)])

        @pl.when(i > 0)
        def _():
            pack(r, [run[n : n + 1, block_lanes(r)] for n in range(3)])
            stat_send(r).start()

        return 0

    lax.fori_loop(0, 5, block, 0)

    def late_block(i, _):
        @pl.when(i == 2)
        def _():
            for r in (1, 7, 2, 6):
                stat_send(r).wait_recv()
            own = [run[n : n + 1, 0:T] for n in range(3)]
            pack(0, own)
            merged = merge([sto[0]] + [sti[32 + r] for r in (1, 7, 2, 6)])
            for n in range(3):
                sto[0, 2 * n : 2 * n + 2, :] = merged[n]
            for d in (3, 5, 2, 6, 1, 7):
                total_send(0, d).start()
            z_step(4, 0)
            for kind in range(3):
                total_send(kind, 4).start()

        r = pick(i, [3, 5, 4])
        near_piece(r, False)
        used, s = near_slot(r)

        @pl.when((i < 2) & used)
        def _():
            near_products(r, s)

        @pl.when(x >= 1)
        def _():
            piece([r], 1, [(1, 1), (2, 2)])

        pack(r, [run[n : n + 1, block_lanes(r)] for n in range(3)])

        for kind in (1, 2):

            @pl.when(i == kind - 1)
            def _():
                for d in (3, 5, 2, 6, 1, 7):
                    total_send(kind, d).start()

        return 0

    lax.fori_loop(0, 3, late_block, 0)
    for d in (4, 3, 5, 2, 6, 1, 7):
        total_send(3, d).start()


    used, s_zero = near_slot(4)

    @pl.when(used)
    def _():
        near_products(4, s_zero)

    @pl.when(x >= 1)
    def _():
        def body(i, _):
            far_products(pl.ds(pl.multiple_of(i * 2 * T, 2 * T), 2 * T))
            return 0

        lax.fori_loop(0, 4, body, 0)


    pltpu.make_async_copy(
        sti.at[pl.ds(0, 4 * (Z - 1))], sti.at[pl.ds(0, 4 * (Z - 1))], fn_r.at[0]
    ).wait()
    for r in range(Z):
        parts = [sto[0] if r == 0 else sti[r]]
        for kind in (1, 2, 3):
            parts.append(sto[r] if far_blocks[kind - 1] == r else sti[kind * Z + r])
        top, total, moment = merge(parts)
        inverse = 1.0 / total
        for n, value in enumerate((top, inverse, moment * inverse)):
            fin[n : n + 1, r * T : (r + 1) * T] = jnp.concatenate([value[0:1, :], value[1:2, :]], axis=1)

    def z_sum(d, i, what, h):
        return copy(
            zs.at[d, i, what, h], zr.at[d, i, what, h], za_s.at[d, i, what, h], za_r.at[d, i, what, h],
            z_right if d == 0 else z_left,
        )

    def z_part(r, what, h):
        rows = slice(h * 128, (h + 1) * 128)
        later = slice(HD + h * 128, HD + (h + 1) * 128)
        lanes = slice(r * T, (r + 1) * T)
        scale = jnp.exp2((run[0:1, lanes] - fin[0:1, lanes]) * ALPHA) * fin[1:2, lanes]
        if what == 0:
            return accv[rows, lanes] * scale
        return (accw[rows, lanes] - fin[2:3, lanes] * accv[later, lanes]) * (scale * INV_ROOT)

    def z_add(i, order=(1, 0)):
        for short in order:
            for h in range(1):
                for d in range(2):
                    what = 1 - d if short else d
                    r = 4 + i if d == 0 else 4 - i
                    part = z_part(r, what, h)
                    if i > short:
                        z_sum(d, i - 1, what, h).wait_recv()
                        part = part + zr[d, i - 1, what, h].astype(F32)
                    zs[d, i, what, h] = part.astype(BF16)
                    send(z_sum(d, i, what, h))

    def sib_send(s):
        return copy(sbs.at[s], sbr.at[s], sb_s.at[s], sb_r.at[s], sib)

    mine = pl.ds(pl.multiple_of(core * T, T), T)
    other = pl.ds(pl.multiple_of((1 - core) * T, T), T)

    def scale_left(which, lanes, valid):
        scale = jnp.exp2((pst[which, 0:1, lanes] - fin[0:1, lanes]) * ALPHA) * fin[1:2, lanes]
        if valid is not None:
            scale = jnp.where(valid, scale, 0.0)
        root = scale * INV_ROOT
        shift = root * (pst[which, 1:2, lanes] - fin[2:3, lanes])
        q = qt[:, lanes].astype(F32)
        left_e[0:HD, lanes] = (gt[:, lanes].astype(F32) * scale).astype(BF16)
        left_e[HD:, lanes] = (q * shift).astype(BF16)
        left_t[:, lanes] = (q * root).astype(BF16)

    def sib_half(s):
        sbs[s] = kacc[s, :, other].astype(BF16)
        send(sib_send(s))

    def key_products(s, rows, lanes):
        kacc[s] = dot_nt(left_e[:, lanes], eb[rows, lanes])
        kacc[s, HD:, :] += dot_nt(left_t[:, lanes], tb[rows, lanes])

    def far_key(s):
        @pl.when(x >= s)
        def _():
            rows = slice(s * C, (s + 1) * C)
            key_products(s, rows, slice(0, Z * T))

        @pl.when(x < s)
        def _():
            kacc[s] = jnp.zeros((2 * HD, C), F32)

        sib_half(s)

    def own_part(s, what):
        rows = slice(what * HD, (what + 1) * HD)
        return kacc[s, rows, mine] + sbr[s, rows, :].astype(F32)

    x_target = [x_right, x_left, x_left, x_left, x_right, x_right]

    def x_sum(i):
        return copy(xs.at[i], xr.at[i], xr_s.at[i], xr_r.at[i], x_target[i])

    def x_send(i, part):
        xs[i] = part.astype(BF16)
        send(x_sum(i))

    z_add(0, (0,))
    z_add(1, (1,))
    for r in (3, 5, 4):
        prepare_queries(r)

    @pl.when(x >= 1)
    def _():
        scale_left(1, slice(0, Z * T), None)

    far_key(2)
    far_key(1)
    sib_send(2).wait_recv()
    x_send(0, own_part(2, 0))
    x_send(1, own_part(2, 1))
    z_add(1, (0,))

    @pl.when(x == X - 1)
    def _():
        scale_left(0, upper, jnp.logical_not(own_lanes)[:, upper])
        key_products(3, slice(0, C), upper)

    @pl.when(x < X - 1)
    def _():
        kacc[3] = jnp.zeros((2 * HD, C), F32)

    sib_half(3)
    sib_send(1).wait_recv()
    x_send(2, own_part(1, 0))
    sib_send(3).wait_recv()
    x_send(5, own_part(3, 1))
    z_add(2)
    scale_left(0, slice(0, Z * T), own_lanes)
    key_products(0, slice(0, C), slice(0, Z * T))
    sib_half(0)
    x_sum(1).wait_recv()
    x_send(3, own_part(1, 1) + xr[1].astype(F32))
    x_sum(0).wait_recv()
    x_send(4, own_part(3, 0) + xr[0].astype(F32))
    z_add(3)

    def leave(i):
        return pltpu.make_async_copy(out_v.at[i], out_ref.at[i], out_s.at[i])

    sib_send(0).wait_recv()
    for what, near in ((0, (2, 4)), (1, (3, 5))):
        part = own_part(0, what)
        for i in near:
            x_sum(i).wait_recv()
            part = part + xr[i].astype(F32)
        out_v[3 - what] = part.T.astype(BF16)
        leave(3 - what).start()

    for hops in (*q_right, *q_left, *g_right, *g_left):
        for op in hops:
            op.wait_send()
    for op in (*k_sib, *v_sib, k_right, v_right, k_left, v_left, k_far, v_far):
        op.wait_send()
    for r in (1, 7, 2, 6):
        stat_send(r).wait_send()
    pltpu.make_async_copy(
        sti.at[pl.ds(0, 4 * (Z - 1))], sti.at[pl.ds(0, 4 * (Z - 1))], fn_s.at[0]
    ).wait()
    for op in started:
        op.wait_send()

    for what in range(2):
        halves = []
        for h in range(1):
            part = z_part(0, what, h)
            for d in range(2):
                z_sum(d, 3, what, h).wait_recv()
                part = part + zr[d, 3, what, h].astype(F32)
            halves.append(part)
        out_v[what] = jnp.concatenate(halves, axis=0).T.astype(BF16)
        leave(what).start()
    for i in range(4):
        leave(i).wait()


def hand_on(all_ref, *outs):
    for i, out in enumerate(outs):
        out[...] = all_ref[i]


def per_device(queries, keys, values, out_grad, segments):
    place = pl.BlockSpec(memory_space=pl.ANY)
    vmem = pl.BlockSpec(memory_space=pltpu.VMEM)
    dma = pltpu.SemaphoreType.DMA
    sums = pl.pallas_call(
        kernel,
        out_shape=jax.ShapeDtypeStruct((4, T, HD), BF16),
        in_specs=[place] * 5,
        out_specs=place,
        scratch_shapes=[
            pltpu.VMEM((T // HD, HD), jnp.int32),
            pltpu.VMEM((SEG_ROWS, HD), F32),
            pltpu.VMEM((4, T, HD), BF16),
            pltpu.VMEM((Z, T + SEG_ROWS, HD), BF16),
            pltpu.VMEM((Z, T, HD), BF16),
            pltpu.VMEM((HD, Z * T), BF16),
            pltpu.VMEM((HD, Z * T), BF16),
            pltpu.VMEM((X, 2, T + SEG_ROWS, HD), BF16),
            pltpu.VMEM((X, 2, T, HD), BF16),
            pltpu.VMEM((2 * HD, X * C), BF16),
            pltpu.VMEM((3 * C, Z * T), BF16),
            pltpu.VMEM((3 * C, Z * T), BF16),
            pltpu.VMEM((2, 4, T, T), F32),
            pltpu.VMEM((2, 4, T, T), F32),
            pltpu.VMEM((2, 8, Z * T), F32),
            pltpu.VMEM((8, Z * T), F32),
            pltpu.VMEM((2 * HD, Z * T), F32),
            pltpu.VMEM((HD, Z * T), F32),
            pltpu.VMEM((2 * HD, Z * T), BF16),
            pltpu.VMEM((HD, Z * T), BF16),
            pltpu.VMEM((X, 2 * HD, C), F32),
            pltpu.VMEM((X, 16, T), F32),
            pltpu.VMEM((Z, 8, HD), F32),
            pltpu.VMEM((5 * Z, 8, HD), F32),
            pltpu.VMEM((8, Z * T), F32),
            pltpu.VMEM((2, 4, 2, 1, HD // 1, T), BF16),
            pltpu.VMEM((2, 4, 2, 1, HD // 1, T), BF16),
            pltpu.VMEM((X, 2 * HD, T), BF16),
            pltpu.VMEM((X, 2 * HD, T), BF16),
            pltpu.VMEM((6, HD, T), BF16),
            pltpu.VMEM((6, HD, T), BF16),
            dma((Z, 1)), dma((Z, 1)), dma((Z, 1)), dma((Z, 1)),
            dma((14,)), dma((14,)),
            dma((Z,)), dma((Z,)), dma((1,)), dma((1,)),
            dma((2, 4, 2, 1)), dma((2, 4, 2, 1)),
            dma((X,)), dma((X,)), dma((6,)), dma((6,)), dma((5,)), dma((4,)),
        ],
        compiler_params=pltpu.CompilerParams(
            collective_id=0, has_side_effects=True, vmem_limit_bytes=58 * 1024 * 1024
        ),
        cost_estimate=pl.CostEstimate(
            flops=4 * 10**9, bytes_accessed=600_000, transcendentals=2 * 10**6
        ),
    )(queries, keys, values, out_grad, segments.reshape(T // HD, HD))
    return tuple(sums[i] for i in range(4))


def solution(mesh):
    rows = P(("dp", "ctx"), None)
    return jax.shard_map(
        per_device,
        mesh=mesh,
        in_specs=(rows, rows, rows, rows, P(("dp", "ctx"))),
        out_specs=(rows, rows, rows, rows),
        check_vma=False,
    )
```

```python
import functools
import math

import jax
import jax.numpy as jnp
from jax import lax
from jax.experimental import pallas as pl
from jax.experimental.pallas import tpu as pltpu
from jax.sharding import PartitionSpec as P

MESH = pl.DeviceIdType.MESH
HD = 128
X, Z = 4, 8
T = 256
C = 2 * T
SEG_ROWS = 16
NEG = -1e30
INV_ROOT = 1.0 / math.sqrt(HD)
ALPHA = INV_ROOT * math.log2(math.e)
F32 = jnp.float32
BF16 = jnp.bfloat16
NT = (((1,), (1,)), ((), ()))


def dot_nt(a, b):
    return lax.dot_general(a, b, NT, preferred_element_type=F32)


def dot(a, b):
    return jnp.dot(a, b, preferred_element_type=F32)


def pick(index, values):
    result = values[-1]
    for i in range(len(values) - 2, -1, -1):
        result = jnp.where(index == i, values[i], result)
    return result


def kernel(
    q_ref, k_ref, v_ref, g_ref, seg_ref, out_ref,
    segi, segf, out_v, qs, gs, qt, gt, ks, vs, vkt, eb, tb, sbuf, dbuf, pst, run, accv, accw,
    left_e, left_t, kacc, cnt, sto, sti, fin, zs, zr, sbs, sbr, xs, xr,
    zq_s, zq_r, zg_s, zg_r, kv_s, kv_r, st_s, st_r, fn_s, fn_r,
    za_s, za_r, sb_s, sb_r, xr_s, xr_r, in_s, out_s,
):
    ctx = lax.axis_index("ctx")
    x = ctx // (2 * Z)
    z = (ctx // 2) % Z
    core = ctx % 2

    def dev(xx, zz, cc):
        return {"ctx": ((xx + X) % X) * (2 * Z) + ((zz + Z) % Z) * 2 + cc}

    sib = dev(x, z, 1 - core)
    z_right, z_left = dev(x, z + 1, core), dev(x, z - 1, core)
    x_right, x_left = dev(x + 1, z, core), dev(x - 1, z, core)

    barrier = pltpu.get_barrier_semaphore()
    for peer in (z_right, z_left, x_right, x_left, sib):
        pl.semaphore_signal(barrier, inc=1, device_id=peer, device_id_type=MESH)

    loads = [
        pltpu.make_async_copy(src, dst, in_s.at[i])
        for i, (src, dst) in enumerate((
            (seg_ref, segi),
            (q_ref, qs.at[0, 0:T, :]),
            (k_ref, ks.at[0, core, 0:T, :]),
            (v_ref, vs.at[0, core]),
            (g_ref, gs.at[0]),
        ))
    ]
    for op in loads:
        op.start()
    segf[...] = jnp.zeros_like(segf)
    run[0:1, :] = jnp.full((1, Z * T), NEG, F32)
    run[1:8, :] = jnp.zeros((7, Z * T), F32)
    loads[0].wait()
    segf[0 : T // HD, :] = segi[...].astype(F32)
    seg_rows = segf[...].astype(BF16)
    qs[0, T : T + SEG_ROWS, :] = seg_rows
    ks[0, core, T : T + SEG_ROWS, :] = seg_rows
    for op in loads[1:]:
        op.wait()

    pl.semaphore_wait(barrier, 5)

    def copy(src, dst, send, recv, target):
        return pltpu.make_async_remote_copy(
            src_ref=src, dst_ref=dst, send_sem=send, recv_sem=recv,
            device_id=target, device_id_type=MESH,
        )

    started = []

    def send(op):
        op.start()
        started.append(op)

    half = (slice(0, T + SEG_ROWS),)

    def q_hop(src, dst, target, h):
        return copy(
            qs.at[src, half[h], :], qs.at[dst, half[h], :], zq_s.at[dst, h], zq_r.at[dst, h], target
        )

    def g_hop(src, dst, target, h):
        rows = slice(h * 256, (h + 1) * 256)
        return copy(gs.at[src, rows, :], gs.at[dst, rows, :], zg_s.at[dst, h], zg_r.at[dst, h], target)

    def k_hop(i, src, dst, target):
        return copy(ks.at[src, core], ks.at[dst, core], kv_s.at[i], kv_r.at[i], target)

    def v_hop(i, src, dst, target):
        return copy(vs.at[src, core], vs.at[dst, core], kv_s.at[i], kv_r.at[i], target)

    q_right = [[q_hop(j, j + 1, z_right, h) for h in range(1)] for j in range(4)]
    q_left = [[q_hop((8 - j) % 8, 7 - j, z_left, h) for h in range(1)] for j in range(3)]
    g_right = [[g_hop(j, j + 1, z_right, h) for h in range(1)] for j in range(3)]
    g_left = [[g_hop((8 - j) % 8, 7 - j, z_left, h) for h in range(1)] for j in range(4)]
    k_sib = [k_hop(s, s, s, sib) for s in range(4)]
    v_sib = [v_hop(4 + s, s, s, sib) for s in range(4)]
    k_right, v_right = k_hop(8, 0, 1, x_right), v_hop(9, 0, 1, x_right)
    k_left, v_left = k_hop(10, 0, 3, x_left), v_hop(11, 0, 3, x_left)
    k_far, v_far = k_hop(12, 1, 2, x_right), v_hop(13, 3, 2, x_left)

    for op in (q_right[0][0], g_left[0][0], k_right, v_left, k_sib[0], v_sib[0]):
        op.start()
    for h in range(1, 1):
        q_right[0][h].start()
        g_left[0][h].start()
    v_right.start()
    k_left.start()
    for h in range(1):
        g_right[0][h].start()
        q_left[0][h].start()

    def z_step(j, which):
        for h in range(1):
            for hops in ((q_right, g_left), (g_right, q_left))[which]:
                if j <= len(hops):
                    hops[j - 1][h].wait_recv()
                if j < len(hops):
                    hops[j][h].start()

    doc16 = lax.broadcasted_iota(jnp.int32, (16, HD), 0).astype(F32)

    def prepare_keys(s):
        below = jnp.zeros((16, HD), F32)
        for c in range(2):
            lanes = slice(s * C + c * T, s * C + (c + 1) * T)
            vkt[0:HD, lanes] = vs[s, c].T
            vkt[HD:, lanes] = ks[s, c, 0:T, :].T
            seg = ks[s, c, T : T + SEG_ROWS, :].astype(F32)
            for h in range(T // HD):
                below += jnp.where(seg[h : h + 1, :] < doc16, 1.0, 0.0)
        cnt[s] = jnp.broadcast_to(jnp.sum(below, axis=1, keepdims=True), (16, T))

    def prepare_queries(r):
        qt[:, r * T : (r + 1) * T] = qs[r, 0:T, :].T
        gt[:, r * T : (r + 1) * T] = gs[r].T

    key_row = lax.broadcasted_iota(jnp.int32, (T, T), 0).astype(F32)
    query_lane = lax.broadcasted_iota(jnp.int32, (1, T), 1).astype(F32)
    doc_q = lax.broadcasted_iota(jnp.int32, (16, T), 0).astype(F32)

    def near_slot(r):
        own = (r == 0) | (r > z)
        used = own | ((x == X - 1) & (r >= 4))
        return used, jnp.where(own, 0, 3)

    def block_lanes(r):
        return pl.ds(pl.multiple_of(r * T, T), T)

    def piece(blocks, which, chunks, diagonal=False):
        tops, lows = [], []
        for n, r in enumerate(blocks):
            seg = qs[r, T : T + SEG_ROWS, :].astype(F32)
            same = jnp.concatenate([seg[0:1, :], seg[1:2, :]], axis=1) == doc_q
            low = [jnp.sum(jnp.where(same, cnt[s], 0.0), axis=0, keepdims=True) for _, s in chunks]
            lows.append([jnp.where(x >= 2, v, 1e9) if u == 2 else v for v, (u, _) in zip(low, chunks)])
            tops.append(run[0:1, block_lanes(r)])
        parts = [(i, s, c, u * C + c * T) for i, (u, s) in enumerate(chunks) for c in range(2)]
        for b, (i, s, c, row) in enumerate(parts):
            for n, r in enumerate(blocks):
                sc = dot_nt(ks[s, c, 0:T, :], qs[r, 0:T, :])
                allowed = key_row >= lows[n][i] - c * T
                if diagonal:
                    allowed = allowed & (key_row <= query_lane + ((core - c) * T).astype(F32))
                sc = jnp.where(allowed, sc, NEG)
                sbuf[n, b] = sc
                tops[n] = jnp.maximum(tops[n], jnp.max(sc, axis=0, keepdims=True))
        totals = [jnp.zeros((1, T), F32) for _ in blocks]
        moments = [jnp.zeros((1, T), F32) for _ in blocks]
        for b, (i, s, c, row) in enumerate(parts):
            for n, r in enumerate(blocks):
                e = jnp.exp2((sbuf[n, b] - tops[n]) * ALPHA)
                weighted = e * dot_nt(vs[s, c], gs[r])
                eb[row : row + T, block_lanes(r)] = e.astype(BF16)
                sbuf[n, b] = e
                dbuf[n, b] = weighted
                totals[n] += jnp.sum(e, axis=0, keepdims=True)
                moments[n] += jnp.sum(weighted, axis=0, keepdims=True)
        means = [moment / jnp.maximum(total, 1e-30) for moment, total in zip(moments, totals)]
        for b, (i, s, c, row) in enumerate(parts):
            for n, r in enumerate(blocks):
                tb[row : row + T, block_lanes(r)] = (dbuf[n, b] - sbuf[n, b] * means[n]).astype(BF16)
        for n, r in enumerate(blocks):
            lanes = block_lanes(r)
            pst[which, 0:1, lanes] = tops[n]
            pst[which, 1:2, lanes] = means[n]
            keep = jnp.exp2((run[0:1, lanes] - tops[n]) * ALPHA)
            run[0:1, lanes] = tops[n]
            run[1:2, lanes] = run[1:2, lanes] * keep + totals[n]
            run[2:3, lanes] = run[2:3, lanes] * keep + moments[n]

    def near_products(r, s):
        lanes = block_lanes(r)
        keys = pl.ds(pl.multiple_of(s * C, C), C)
        part_v = dot(vkt[:, keys], eb[0:C, lanes])
        part_t = dot(vkt[HD:, keys], tb[0:C, lanes])
        accv[:, lanes] = part_v
        accw[:, lanes] = part_t + pst[0, 1:2, lanes] * part_v[HD:, :]

    def far_products(lanes):
        part_v = dot(vkt[:, C : 3 * C], eb[C : 3 * C, lanes])
        part_t = dot(vkt[HD:, C : 3 * C], tb[C : 3 * C, lanes])
        keep = jnp.exp2((pst[0, 0:1, lanes] - run[0:1, lanes]) * ALPHA)
        accv[:, lanes] = accv[:, lanes] * keep + part_v
        accw[:, lanes] = accw[:, lanes] * keep + part_t + pst[1, 1:2, lanes] * part_v[HD:, :]

    def near_piece(r, multiply):
        used, s = near_slot(r)

        @pl.when(used)
        def _():
            piece([r], 0, [(0, s)])
            if multiply:
                near_products(r, s)

        @pl.when(jnp.logical_not(used))
        def _():
            lanes = block_lanes(r)
            eb[0:C, lanes] = jnp.zeros((C, T), BF16)
            tb[0:C, lanes] = jnp.zeros((C, T), BF16)
            pst[0, 0:1, lanes] = jnp.full((1, T), NEG, F32)
            pst[0, 1:2, lanes] = jnp.zeros((1, T), F32)
            accv[:, lanes] = jnp.zeros((2 * HD, T), F32)
            accw[:, lanes] = jnp.zeros((HD, T), F32)

    lane_block = lax.broadcasted_iota(jnp.int32, (1, Z * T), 1) // T
    own_lanes = (lane_block == 0) | (lane_block > z)
    upper = slice(4 * T, Z * T)

    def pack(i, values):
        for n in range(3):
            for h in range(2):
                sto[i, 2 * n + h : 2 * n + h + 1, :] = values[n][:, h * HD : (h + 1) * HD]

    def merge(parts):
        top = functools.reduce(jnp.maximum, [p[0:2, :] for p in parts])
        scales = [jnp.exp2((p[0:2, :] - top) * ALPHA) for p in parts]
        total = sum(p[2:4, :] * scale for p, scale in zip(parts, scales))
        moment = sum(p[4:6, :] * scale for p, scale in zip(parts, scales))
        return top, total, moment

    def stat_send(r):
        return copy(sto.at[r], sti.at[32 + r], st_s.at[r], st_r.at[r], dev(x, z - r, core))

    far_blocks = (3, 5, 4)

    def total_send(kind, d):
        r = 0 if kind == 0 else far_blocks[kind - 1]
        slot = kind * Z + (d + r) % Z
        return copy(sto.at[r], sti.at[slot], fn_s.at[0], fn_r.at[0], dev(x, z + d, core))

    prepare_queries(0)
    k_sib[0].wait_recv()
    v_sib[0].wait_recv()
    prepare_keys(0)
    piece([0], 0, [(0, 0)], diagonal=True)
    near_products(0, 0)

    z_step(1, 0)
    k_right.wait_recv()
    k_far.start()
    k_sib[1].start()
    v_left.wait_recv()
    v_far.start()
    v_sib[3].start()
    z_step(1, 1)
    v_right.wait_recv()
    v_sib[1].start()
    k_left.wait_recv()
    k_sib[3].start()
    prepare_queries(1)
    prepare_queries(7)
    z_step(2, 0)
    for s in (1, 3):
        k_sib[s].wait_recv()
        v_sib[s].wait_recv()
        prepare_keys(s)

    def early(i, _):
        @pl.when(i == 1)
        def _():
            k_far.wait_recv()
            k_sib[2].start()
            v_far.wait_recv()
            v_sib[2].start()

        @pl.when(i == 2)
        def _():
            z_step(2, 1)
            prepare_queries(2)
            prepare_queries(6)

        near_piece(pick(i, [1, 7, 2, 6]), True)
        return 0

    lax.fori_loop(0, 4, early, 0)
    z_step(3, 0)
    k_sib[2].wait_recv()
    v_sib[2].wait_recv()
    prepare_keys(2)

    def block(i, _):
        r = pick(i, [0, 1, 7, 2, 6])

        @pl.when(x >= 1)
        def _():
            piece([r], 1, [(1, 1), (2, 2)])

        @pl.when(i > 0)
        def _():
            pack(r, [run[n : n + 1, block_lanes(r)] for n in range(3)])
            stat_send(r).start()

        return 0

    lax.fori_loop(0, 5, block, 0)
    z_step(3, 1)

    def late_block(i, _):
        @pl.when(i == 2)
        def _():
            for r in (1, 7, 2, 6):
                stat_send(r).wait_recv()
            own = [run[n : n + 1, 0:T] for n in range(3)]
            pack(0, own)
            merged = merge([sto[0]] + [sti[32 + r] for r in (1, 7, 2, 6)])
            for n in range(3):
                sto[0, 2 * n : 2 * n + 2, :] = merged[n]
            for d in (3, 5, 2, 6, 1, 7):
                total_send(0, d).start()
            z_step(4, 0)
            for kind in range(3):
                total_send(kind, 4).start()

        r = pick(i, [3, 5, 4])
        near_piece(r, False)
        used, s = near_slot(r)

        @pl.when((i < 2) & used)
        def _():
            near_products(r, s)

        @pl.when(x >= 1)
        def _():
            piece([r], 1, [(1, 1), (2, 2)])

        pack(r, [run[n : n + 1, block_lanes(r)] for n in range(3)])

        for kind in (1, 2):

            @pl.when(i == kind - 1)
            def _():
                for d in (3, 5, 2, 6, 1, 7):
                    total_send(kind, d).start()

        return 0

    lax.fori_loop(0, 3, late_block, 0)
    for d in (4, 3, 5, 2, 6, 1, 7):
        total_send(3, d).start()


    used, s_zero = near_slot(4)

    @pl.when(used)
    def _():
        near_products(4, s_zero)

    @pl.when(x >= 1)
    def _():
        def body(i, _):
            far_products(pl.ds(pl.multiple_of(i * 2 * T, 2 * T), 2 * T))
            return 0

        lax.fori_loop(0, 4, body, 0)

    for r in (3, 5, 4):
        prepare_queries(r)

    pltpu.make_async_copy(
        sti.at[pl.ds(0, 4 * (Z - 1))], sti.at[pl.ds(0, 4 * (Z - 1))], fn_r.at[0]
    ).wait()
    for r in range(Z):
        parts = [sto[0] if r == 0 else sti[r]]
        for kind in (1, 2, 3):
            parts.append(sto[r] if far_blocks[kind - 1] == r else sti[kind * Z + r])
        top, total, moment = merge(parts)
        inverse = 1.0 / total
        for n, value in enumerate((top, inverse, moment * inverse)):
            fin[n : n + 1, r * T : (r + 1) * T] = jnp.concatenate([value[0:1, :], value[1:2, :]], axis=1)

    def z_sum(d, i, what, h):
        return copy(
            zs.at[d, i, what, h], zr.at[d, i, what, h], za_s.at[d, i, what, h], za_r.at[d, i, what, h],
            z_right if d == 0 else z_left,
        )

    def z_part(r, what, h):
        rows = slice(h * 128, (h + 1) * 128)
        later = slice(HD + h * 128, HD + (h + 1) * 128)
        lanes = slice(r * T, (r + 1) * T)
        scale = jnp.exp2((run[0:1, lanes] - fin[0:1, lanes]) * ALPHA) * fin[1:2, lanes]
        if what == 0:
            return accv[rows, lanes] * scale
        return (accw[rows, lanes] - fin[2:3, lanes] * accv[later, lanes]) * (scale * INV_ROOT)

    def z_add(i, order=(1, 0)):
        for short in order:
            for h in range(1):
                for d in range(2):
                    what = 1 - d if short else d
                    r = 4 + i if d == 0 else 4 - i
                    part = z_part(r, what, h)
                    if i > short:
                        z_sum(d, i - 1, what, h).wait_recv()
                        part = part + zr[d, i - 1, what, h].astype(F32)
                    zs[d, i, what, h] = part.astype(BF16)
                    send(z_sum(d, i, what, h))

    def sib_send(s):
        return copy(sbs.at[s], sbr.at[s], sb_s.at[s], sb_r.at[s], sib)

    mine = pl.ds(pl.multiple_of(core * T, T), T)
    other = pl.ds(pl.multiple_of((1 - core) * T, T), T)

    def scale_left(which, lanes, valid):
        scale = jnp.exp2((pst[which, 0:1, lanes] - fin[0:1, lanes]) * ALPHA) * fin[1:2, lanes]
        if valid is not None:
            scale = jnp.where(valid, scale, 0.0)
        root = scale * INV_ROOT
        shift = root * (pst[which, 1:2, lanes] - fin[2:3, lanes])
        q = qt[:, lanes].astype(F32)
        left_e[0:HD, lanes] = (gt[:, lanes].astype(F32) * scale).astype(BF16)
        left_e[HD:, lanes] = (q * shift).astype(BF16)
        left_t[:, lanes] = (q * root).astype(BF16)

    def sib_half(s):
        sbs[s] = kacc[s, :, other].astype(BF16)
        send(sib_send(s))

    def key_products(s, rows, lanes):
        kacc[s] = dot_nt(left_e[:, lanes], eb[rows, lanes])
        kacc[s, HD:, :] += dot_nt(left_t[:, lanes], tb[rows, lanes])

    def far_key(s):
        @pl.when(x >= s)
        def _():
            rows = slice(s * C, (s + 1) * C)
            key_products(s, rows, slice(0, Z * T))

        @pl.when(x < s)
        def _():
            kacc[s] = jnp.zeros((2 * HD, C), F32)

        sib_half(s)

    def own_part(s, what):
        rows = slice(what * HD, (what + 1) * HD)
        return kacc[s, rows, mine] + sbr[s, rows, :].astype(F32)

    x_target = [x_right, x_left, x_left, x_left, x_right, x_right]

    def x_sum(i):
        return copy(xs.at[i], xr.at[i], xr_s.at[i], xr_r.at[i], x_target[i])

    def x_send(i, part):
        xs[i] = part.astype(BF16)
        send(x_sum(i))

    z_add(0, (0,))
    z_add(1, (1,))

    @pl.when(x >= 1)
    def _():
        scale_left(1, slice(0, Z * T), None)

    far_key(2)
    far_key(1)
    sib_send(2).wait_recv()
    x_send(0, own_part(2, 0))
    x_send(1, own_part(2, 1))
    z_add(1, (0,))

    @pl.when(x == X - 1)
    def _():
        scale_left(0, upper, jnp.logical_not(own_lanes)[:, upper])
        key_products(3, slice(0, C), upper)

    @pl.when(x < X - 1)
    def _():
        kacc[3] = jnp.zeros((2 * HD, C), F32)

    sib_half(3)
    sib_send(1).wait_recv()
    x_send(2, own_part(1, 0))
    sib_send(3).wait_recv()
    x_send(5, own_part(3, 1))
    z_add(2)
    scale_left(0, slice(0, Z * T), own_lanes)
    key_products(0, slice(0, C), slice(0, Z * T))
    sib_half(0)
    x_sum(1).wait_recv()
    x_send(3, own_part(1, 1) + xr[1].astype(F32))
    x_sum(0).wait_recv()
    x_send(4, own_part(3, 0) + xr[0].astype(F32))
    z_add(3)

    def leave(i):
        return pltpu.make_async_copy(out_v.at[i], out_ref.at[i], out_s.at[i])

    sib_send(0).wait_recv()
    for what, near in ((0, (2, 4)), (1, (3, 5))):
        part = own_part(0, what)
        for i in near:
            x_sum(i).wait_recv()
            part = part + xr[i].astype(F32)
        out_v[3 - what] = part.T.astype(BF16)
        leave(3 - what).start()

    for hops in (*q_right, *q_left, *g_right, *g_left):
        for op in hops:
            op.wait_send()
    for op in (*k_sib, *v_sib, k_right, v_right, k_left, v_left, k_far, v_far):
        op.wait_send()
    for r in (1, 7, 2, 6):
        stat_send(r).wait_send()
    pltpu.make_async_copy(
        sti.at[pl.ds(0, 4 * (Z - 1))], sti.at[pl.ds(0, 4 * (Z - 1))], fn_s.at[0]
    ).wait()
    for op in started:
        op.wait_send()

    for what in range(2):
        halves = []
        for h in range(1):
            part = z_part(0, what, h)
            for d in range(2):
                z_sum(d, 3, what, h).wait_recv()
                part = part + zr[d, 3, what, h].astype(F32)
            halves.append(part)
        out_v[what] = jnp.concatenate(halves, axis=0).T.astype(BF16)
        leave(what).start()
    for i in range(4):
        leave(i).wait()


def hand_on(all_ref, *outs):
    for i, out in enumerate(outs):
        out[...] = all_ref[i]


def per_device(queries, keys, values, out_grad, segments):
    place = pl.BlockSpec(memory_space=pl.ANY)
    vmem = pl.BlockSpec(memory_space=pltpu.VMEM)
    dma = pltpu.SemaphoreType.DMA
    sums = pl.pallas_call(
        kernel,
        out_shape=jax.ShapeDtypeStruct((4, T, HD), BF16),
        in_specs=[place] * 5,
        out_specs=place,
        scratch_shapes=[
            pltpu.VMEM((T // HD, HD), jnp.int32),
            pltpu.VMEM((SEG_ROWS, HD), F32),
            pltpu.VMEM((4, T, HD), BF16),
            pltpu.VMEM((Z, T + SEG_ROWS, HD), BF16),
            pltpu.VMEM((Z, T, HD), BF16),
            pltpu.VMEM((HD, Z * T), BF16),
            pltpu.VMEM((HD, Z * T), BF16),
            pltpu.VMEM((X, 2, T + SEG_ROWS, HD), BF16),
            pltpu.VMEM((X, 2, T, HD), BF16),
            pltpu.VMEM((2 * HD, X * C), BF16),
            pltpu.VMEM((3 * C, Z * T), BF16),
            pltpu.VMEM((3 * C, Z * T), BF16),
            pltpu.VMEM((2, 4, T, T), F32),
            pltpu.VMEM((2, 4, T, T), F32),
            pltpu.VMEM((2, 8, Z * T), F32),
            pltpu.VMEM((8, Z * T), F32),
            pltpu.VMEM((2 * HD, Z * T), F32),
            pltpu.VMEM((HD, Z * T), F32),
            pltpu.VMEM((2 * HD, Z * T), BF16),
            pltpu.VMEM((HD, Z * T), BF16),
            pltpu.VMEM((X, 2 * HD, C), F32),
            pltpu.VMEM((X, 16, T), F32),
            pltpu.VMEM((Z, 8, HD), F32),
            pltpu.VMEM((5 * Z, 8, HD), F32),
            pltpu.VMEM((8, Z * T), F32),
            pltpu.VMEM((2, 4, 2, 1, HD // 1, T), BF16),
            pltpu.VMEM((2, 4, 2, 1, HD // 1, T), BF16),
            pltpu.VMEM((X, 2 * HD, T), BF16),
            pltpu.VMEM((X, 2 * HD, T), BF16),
            pltpu.VMEM((6, HD, T), BF16),
            pltpu.VMEM((6, HD, T), BF16),
            dma((Z, 1)), dma((Z, 1)), dma((Z, 1)), dma((Z, 1)),
            dma((14,)), dma((14,)),
            dma((Z,)), dma((Z,)), dma((1,)), dma((1,)),
            dma((2, 4, 2, 1)), dma((2, 4, 2, 1)),
            dma((X,)), dma((X,)), dma((6,)), dma((6,)), dma((5,)), dma((4,)),
        ],
        compiler_params=pltpu.CompilerParams(
            collective_id=0, has_side_effects=True, vmem_limit_bytes=58 * 1024 * 1024
        ),
        cost_estimate=pl.CostEstimate(
            flops=4 * 10**9, bytes_accessed=600_000, transcendentals=2 * 10**6
        ),
    )(queries, keys, values, out_grad, segments.reshape(T // HD, HD))
    return tuple(sums[i] for i in range(4))


def solution(mesh):
    rows = P(("dp", "ctx"), None)
    return jax.shard_map(
        per_device,
        mesh=mesh,
        in_specs=(rows, rows, rows, rows, P(("dp", "ctx"))),
        out_specs=(rows, rows, rows, rows),
        check_vma=False,
    )
```
